256 devices in a mesh: pool: 2 (over core), ep: 32 (over y, z), half: 4 (over x).
Axes of the slice: x: 4, y: 4, z: 8, core: 2. Of those that a mesh axis runs over, the one named last changes fastest.
Arguments:
- tokens: bfloat16 [2, 2048, 4096], P('pool', 'ep'), may hold values from -6 to 6
- routes: int32 [2, 2048, 8], P('pool', 'ep'), may hold values from 0 to 31, all different within a row; in each aligned block of 64 rows (0 to 63, 64 to 127, ..., all dimensions but the last counted through in order) at most 32 rows name the same one
- router: bfloat16 [4096, 32], replicated, may hold values from -0.03125 to 0.03125
- w_gate: bfloat16 [32, 4096, 1536], P('ep', None, 'half'), may hold values from -0.09375 to 0.09375
- w_up: bfloat16 [32, 4096, 1536], P('ep', None, 'half'), may hold values from -0.09375 to 0.09375
- w_down: bfloat16 [32, 1536, 4096], P('ep', 'half'), may hold values from -0.625 to 0.625
- norm_gain: float32 [4096], replicated, may hold values from 0.1 to 1.9
- w_kv: bfloat16 [4096, 2048], P('ep', 'half'), may hold values from -0.09375 to 0.09375
- lengths: int32 [2, 32, 2], P(None, 'ep'), may hold values from 1 to 48, 64 in all within a row
- queries: bfloat16 [2, 8192, 2048], P('pool', 'ep', 'half'), may hold values from -150 to 150
- new_keys: bfloat16 [2, 8192, 1024], P('pool', 'ep', 'half'), may hold values from -5 to 5
- new_values: bfloat16 [2, 8192, 1024], P('pool', 'ep', 'half'), may hold values from -6 to 6
- w_out: bfloat16 [2048, 2048], P('half'), may hold values from -0.125 to 0.125
Outputs:
- decoded: bfloat16 [2, 8192, 2048], P('pool', ('ep', 'half'))
The draws below stay inside these ranges and needn't reach their ends.
Inputs may be any that keep to these rules, and one draw needn't show every extreme that they name: `routes`: each token names 8 different experts; within each aligned block of 64 tokens no expert is named by more than 32 tokens. The 2 lengths of a group sum to 64.
All inputs are finite; a program needn't handle non-finite values.
Results may differ from the reference program's by a relative error of at most 0.022.
Values may be sent and summed in bfloat16 or wider, within the bound.
A program may use at most 128 MiB of HBM per device.

```python
import math
import jax
import jax.numpy as jnp
import numpy as np
from jax import lax

D = 4096
FF = 1536
EXPERTS = 32
TOP = 8
HEAD = 128
KV_HEADS = 8
Q_HEADS = 16
D_OUT = 2048
TOK_DEV = 64
PROMPT_GRP = 2
SAMPLES = 128
TOKENS = 2048
CAP = 32
LEN_MOST = 48
ROWS = 8192
N_EP = 32
N_HALF = 4


def decode_inputs(key):
    fresh = jnp.clip(jax.random.normal(jax.random.fold_in(key, 101), (2, ROWS, KV_HEADS, HEAD), jnp.float32), -5.0, 5.0)
    query = jnp.clip(jax.random.normal(jax.random.fold_in(key, 102), (2, ROWS, KV_HEADS, Q_HEADS // KV_HEADS, HEAD), jnp.float32), -5.0, 5.0)
    return (query.reshape(2, ROWS, Q_HEADS * HEAD), fresh.reshape(2, ROWS, KV_HEADS * HEAD))


def draw_queries(key, part):
    return decode_inputs(key)[0].astype(jnp.bfloat16)


def draw_new_keys(key, part):
    return decode_inputs(key)[1].astype(jnp.bfloat16)


def steps_of(stream_key, dims, shards, smallest, high):
    def one(dim, blocks):
        draws = jax.random.uniform(jax.random.fold_in(jax.random.fold_in(stream_key, 6), dim), (blocks,), jnp.float32, smallest / len(shards), high / len(shards))
        return jnp.repeat(jnp.exp(draws), dims[dim] // blocks).reshape((-1,) + (1,) * (len(dims) - dim - 1))

    loudness = one(*shards[0])
    for cut in shards[1:]:
        loudness = loudness * one(*cut)
    return loudness


def split_up(count, total, most, skew):
    portions = [(1 << 20) // math.isqrt(standing ** skew) + 1 for standing in range(2, count + 1)]
    spare, holding = total - most - (count - 1), [1] * (count - 1)
    while spare > 0:
        candidates = [i for i in range(count - 1) if holding[i] < most]
        whole, budget = sum([portions[i] for i in candidates]), spare
        for i in candidates:
            more = min(most - holding[i], max(1, budget * portions[i] // whole), spare)
            holding[i] = holding[i] + more
            spare = spare - more
    return np.array([most] + holding)


def ragged_sizes(stream_key, amount, total, bound, skew):
    if amount == 2:
        one = jax.random.randint(stream_key, (), max(1, total - bound), min(bound, total - 1) + 1)
        return jnp.stack([one, total - one])
    sizes = jnp.asarray(split_up(amount, total, bound, skew), jnp.int32)
    pairs = (amount - 1) // 2
    source_of, taker = sizes[1:1 + 2 * pairs:2], sizes[2:2 + 2 * pairs:2]
    room = jnp.minimum(source_of - 1, bound - taker)
    passed = jax.random.randint(jax.random.fold_in(stream_key, 1), (pairs,), 0, 1 << 20) % (room + 1)
    sizes = sizes.at[1:1 + 2 * pairs:2].set(source_of - passed).at[2:2 + 2 * pairs:2].set(taker + passed)
    return sizes[jax.random.permutation(jax.random.fold_in(stream_key, 2), amount)]


def assign_block(rng, own, number, rows, count, top, bound, slope):
    sequence = jax.random.permutation(rng, count)
    packed, common = portions_of(count, rows * top, bound, slope, True), portions_of(count, rows * top, bound, slope, False)
    places = jnp.arange(count)

    def named(sizes, offset_by):
        used = int((sizes > 0).sum())
        fixed = max(1, used // 4)
        shifted = fixed + (places - fixed + offset_by * (used - fixed)) % max(1, count - fixed)
        return jnp.zeros((count,), jnp.int32).at[sequence[jnp.where(places < fixed, places, shifted)]].set(jnp.asarray(sizes, jnp.int32))

    sizes = jnp.where(number % 4 == 0, named(packed, number // 4), named(common, number - number // 4 - 1))
    mixed = jax.random.permutation(jax.random.fold_in(own, 3), count)
    donor, taker = mixed[0:count // 2 * 2:2], mixed[1:count // 2 * 2:2]
    room = jnp.minimum(sizes[donor] - 1, bound - sizes[taker]) // 2
    room = jnp.where((donor == sequence[0]) | (taker == sequence[0]) | (sizes[taker] == 0), 0, jnp.maximum(room, 0))
    shifted = jax.random.randint(jax.random.fold_in(own, 4), (count // 2,), 0, 1 << 20) % (room + 1)
    sizes = sizes.at[donor].add(-shifted).at[taker].add(shifted)
    labels = jnp.searchsorted(jnp.cumsum(sizes), jnp.arange(rows * top), side="right").astype(jnp.int32)
    table = labels.reshape(top, rows).T
    table = table[jax.random.permutation(jax.random.fold_in(own, 1), rows)]
    offset_by = jax.random.randint(jax.random.fold_in(own, 2), (rows, 1), 0, top)
    return jnp.take_along_axis(table, (jnp.arange(top)[None, :] + offset_by) % top, axis=1)


def portions_of(number_of, total, reach, skew, full):
    portions = [(1 << 20) // math.isqrt(grade ** skew) + 1 for grade in range(1, number_of + 1)]
    largest = reach if full else min(reach, max(-(-total // number_of), total * portions[0] // sum(portions)))
    least = 1 if total - largest >= number_of - 1 else 0
    counts, rest = [largest] + [least] * (number_of - 1), total - largest - least * (number_of - 1)
    while rest > 0:
        candidates = [i for i in range(1, number_of) if counts[i] < largest] or [i for i in range(1, number_of) if counts[i] < reach]
        mass, left = sum([portions[i] for i in candidates]), rest
        for i in candidates:
            extra = min(reach - counts[i], max(1, left * portions[i] // mass), rest)
            counts[i] = counts[i] + extra
            rest = rest - extra
    return np.array(counts)


def normal_values(stream_key, extent, scale, limit, split=(), kind=jnp.bfloat16):
    drawn = scale * jax.random.normal(stream_key, extent, jnp.float32)
    if split:
        drawn = drawn * steps_of(stream_key, extent, split, -0.22, 0.18)
    return jnp.clip(drawn, -limit, limit).astype(kind)


def setup_inputs(seed: int = 0) -> dict:
    splits = jax.random.split(jax.random.key(seed), 14)
    tokens = normal_values(splits[0], (2, TOKENS, D), 1.0, 6.0, ((0, 2), (1, 32)))
    routes_keys = jax.random.split(jax.random.fold_in(splits[1], 1), 2 * TOKENS // TOK_DEV)
    routes_turns = jax.random.permutation(jax.random.fold_in(splits[1], 3), 2 * TOKENS // TOK_DEV)
    routes = jax.vmap(lambda own, number: assign_block(jax.random.fold_in(splits[1], 2), own, number, TOK_DEV, EXPERTS, TOP, CAP, 4))(routes_keys, routes_turns).reshape((2, TOKENS, TOP))
    router = normal_values(splits[2], (D, EXPERTS), (8 * D) ** -0.5, 0.03125)
    w_gate = normal_values(splits[3], (EXPERTS, D, FF), D ** -0.5, 0.09375, ((0, 32), (2, 4)))
    w_up = normal_values(splits[4], (EXPERTS, D, FF), D ** -0.5, 0.09375, ((0, 32), (2, 4)))
    w_down = normal_values(splits[5], (EXPERTS, FF, D), (FF // 16) ** -0.5, 0.625, ((0, 32), (1, 4)))
    norm_gain = jnp.clip(1.0 + 0.18 * jax.random.normal(splits[6], (D,), jnp.float32), 0.1, 1.9)
    w_kv = normal_values(splits[7], (D, 2 * KV_HEADS * HEAD), D ** -0.5, 0.09375, ((0, 32), (1, 4)))
    lengths = jax.vmap(lambda own: ragged_sizes(own, PROMPT_GRP, TOK_DEV, LEN_MOST, 2))(jax.random.split(splits[8], 2 * N_EP)).reshape((2, N_EP, PROMPT_GRP)).astype(jnp.int32)
    queries = draw_queries(jax.random.fold_in(splits[13], 71), 0)
    new_keys = draw_new_keys(jax.random.fold_in(splits[13], 71), 0)
    new_values = normal_values(splits[11], (2, ROWS, KV_HEADS * HEAD), 1.0, 6.0, ((0, 2), (1, 32), (2, 4)))
    w_out = normal_values(splits[12], (Q_HEADS * HEAD, D_OUT), (Q_HEADS * HEAD) ** -0.5, 0.125, ((0, 4),))
    return {"tokens": tokens, "routes": routes, "router": router, "w_gate": w_gate, "w_up": w_up, "w_down": w_down, "norm_gain": norm_gain, "w_kv": w_kv, "lengths": lengths, "queries": queries, "new_keys": new_keys, "new_values": new_values, "w_out": w_out}


def prefill(tokens_set, chosen, router, w_gate, w_up, w_down, norm_gain, w_kv):
    logits = jnp.dot(tokens_set, router, preferred_element_type=jnp.float32)
    picked = jnp.take_along_axis(logits, chosen, axis=1)
    weights = jax.nn.softmax(picked, axis=1).reshape(-1)
    blocks = TOKENS // TOK_DEV
    width = TOK_DEV * TOP
    expert_of = chosen.reshape(blocks, width).astype(jnp.int32)
    onehot = (expert_of[:, :, None] == jnp.arange(EXPERTS, dtype=jnp.int32)[None, None, :]).astype(jnp.int32)
    before = jnp.cumsum(onehot, axis=1) - onehot
    rank = lax.optimization_barrier(jnp.sum(before * onehot, axis=2)).astype(jnp.int32)
    block_index = jnp.broadcast_to(jnp.arange(blocks, dtype=jnp.int32)[:, None], (blocks, width))
    flat_index = block_index * width + jnp.arange(width, dtype=jnp.int32)[None, :]
    table = jnp.full((EXPERTS, blocks, CAP), -1, jnp.int32).at[expert_of, block_index, rank].set(flat_index)
    quarter = FF // N_HALF

    def expert_step(carry, expert):
        entry = table[expert].reshape(-1)
        valid = entry >= 0
        safe = jnp.where(valid, entry, 0).astype(jnp.int32)
        token = (safe // TOP).astype(jnp.int32)
        rows = jnp.where(valid[:, None], tokens_set[token], jnp.zeros((), tokens_set.dtype))
        gate = jnp.dot(rows, w_gate[expert], preferred_element_type=jnp.float32)
        up = jnp.dot(rows, w_up[expert], preferred_element_type=jnp.float32)
        hidden = (jax.nn.silu(gate) * up).astype(jnp.bfloat16)
        down = w_down[expert]
        total = jnp.zeros((rows.shape[0], D), jnp.float32)
        for piece_index in range(N_HALF):
            lower = piece_index * quarter
            piece = jnp.dot(hidden[:, lower:lower + quarter], down[lower:lower + quarter], preferred_element_type=jnp.float32)
            total = total + lax.optimization_barrier(piece.astype(jnp.bfloat16)).astype(jnp.float32)
        result = lax.optimization_barrier(total.astype(jnp.bfloat16)).astype(jnp.float32)
        scale = jnp.where(valid, weights[safe], 0.0)
        return (carry.at[token].add(scale[:, None] * result), None)
    mixed, unused = lax.scan(expert_step, tokens_set.astype(jnp.float32), jnp.arange(EXPERTS, dtype=jnp.int32))
    meansq = lax.optimization_barrier(jnp.mean(mixed * mixed, axis=1, keepdims=True))
    normed = (mixed * lax.rsqrt(meansq + 1e-06) * norm_gain).astype(jnp.bfloat16)
    return jnp.dot(normed, w_kv, preferred_element_type=jnp.float32).astype(jnp.bfloat16)

def attend(block, prompt_lengths, query, fresh_key, fresh_value):
    group_tok = block.shape[0]
    group_rows = query.shape[0]
    ends = jnp.cumsum(prompt_lengths)
    position = jnp.arange(group_tok, dtype=jnp.int32)
    segment = lax.optimization_barrier(jnp.sum((position[:, None] >= ends[None, :]).astype(jnp.int32), axis=1))
    prompt = jnp.arange(group_rows, dtype=jnp.int32) // SAMPLES
    allowed = segment[None, :] == prompt[:, None]
    keys = block[:, :, 0, :].astype(jnp.float32)
    values = block[:, :, 1, :].astype(jnp.float32)
    scale = 1.0 / math.sqrt(HEAD)
    scores = jnp.einsum('rhgd,thd->rhgt', query.astype(jnp.float32), keys) * scale
    scores = jnp.where(allowed[:, None, None, :], scores, -1e+30)
    own = jnp.einsum('rhgd,rhd->rhg', query.astype(jnp.float32), fresh_key.astype(jnp.float32)) * scale
    top = jnp.maximum(lax.optimization_barrier(jnp.max(scores, axis=3)), own)
    spread = jnp.where(allowed[:, None, None, :], jnp.exp(scores - top[..., None]), 0.0)
    self_weight = jnp.exp(own - top)
    total = lax.optimization_barrier(jnp.sum(spread, axis=3)) + self_weight
    probs = (spread / total[..., None]).astype(jnp.bfloat16)
    self_prob = (self_weight / total).astype(jnp.bfloat16)
    mixed = jnp.einsum('rhgt,thd->rhgd', probs.astype(jnp.float32), values)
    mixed = mixed + self_prob.astype(jnp.float32)[..., None] * fresh_value.astype(jnp.float32)[:, :, None, :]
    return mixed.astype(jnp.bfloat16).reshape(group_rows, -1)

def decode(keyvals, prompt_lengths, query_set, key_set, value_set, w_out):
    group_tok = TOKENS // N_EP
    group_rows = PROMPT_GRP * SAMPLES
    heads_group = Q_HEADS // KV_HEADS
    blocks = keyvals.reshape(N_EP, group_tok, KV_HEADS, 2, HEAD)
    query_all = query_set.reshape(N_EP, group_rows, KV_HEADS, heads_group, HEAD)
    key_all = key_set.reshape(N_EP, group_rows, KV_HEADS, HEAD)
    value_all = value_set.reshape(N_EP, group_rows, KV_HEADS, HEAD)

    def group_step(items):
        return attend(items[0], items[1], items[2], items[3], items[4])
    attention = lax.map(group_step, (blocks, prompt_lengths, query_all, key_all, value_all))
    flat = attention.reshape(N_EP * group_rows, Q_HEADS * HEAD)
    return jnp.dot(flat, w_out, preferred_element_type=jnp.float32).astype(jnp.bfloat16)

def reference(tokens, routes, router, w_gate, w_up, w_down, norm_gain, w_kv, lengths, queries, new_keys, new_values, w_out):
    keyvals = [prefill(tokens[which], routes[which], router, w_gate, w_up, w_down, norm_gain, w_kv) for which in range(2)]
    outputs = [decode(keyvals[1 - which], lengths[1 - which], queries[which], new_keys[which], new_values[which], w_out) for which in range(2)]
    return jnp.stack(outputs)
```

```python
import math

import jax
import jax.numpy as jnp
from jax import lax
from jax.experimental import pallas as pl
from jax.experimental.pallas import tpu as pltpu
from jax.sharding import PartitionSpec as P

HEAD = 128
SAMPLES = 128
CAP = 32
SLOTS = 16
MESH = pl.DeviceIdType.MESH
BF16 = jnp.bfloat16
F32 = jnp.float32


def moe_kernel(
    out_rows,
    combine,
    w_gate,
    w_up,
    w_down,
    result,
    w_in,
    w_out,
    mine,
    from_left,
    from_right,
    from_far,
    acc,
    hidden,
    partial,
    inbox,
    done,
    returned,
    piece,
    gathered,
    w_sem,
    local_sem,
    send_sem,
    recv_sem,
    ring_send,
    ring_recv,
    sum_send,
    sum_recv,
    back_local,
    back_send,
    back_recv,
    mix_send,
    mix_recv,
):
    chunks, n_ep, slots, quarter = out_rows.shape
    width = quarter // 2
    ff = w_gate.shape[1]
    half_groups = n_ep // 2
    half_rows = half_groups * slots
    tokens = combine.shape[1]
    ep = lax.axis_index("ep")
    x = lax.axis_index("half")
    right = lax.rem(x + 1, 4)
    left = lax.rem(x + 3, 4)
    far = lax.rem(x + 2, 4)

    loads = [
        pltpu.make_async_copy(w_gate, w_in.at[:, pl.ds(0, ff)], w_sem.at[0]),
        pltpu.make_async_copy(w_up, w_in.at[:, pl.ds(ff, ff)], w_sem.at[1]),
        pltpu.make_async_copy(w_down, w_out, w_sem.at[2]),
    ]
    for load in loads:
        load.start()

    barrier = pltpu.get_barrier_semaphore()

    @pl.loop(1, n_ep)
    def _(i):
        peer = lax.rem(ep + i, n_ep)
        pl.semaphore_signal(barrier, inc=1, device_id={"ep": peer}, device_id_type=MESH)

    for peer in (left, right, far):
        pl.semaphore_signal(barrier, inc=1, device_id={"half": peer}, device_id_type=MESH)
    pl.semaphore_wait(barrier, n_ep + 2)

    def stage(k):
        return k // 2, pl.ds(k % 2 * width, width)

    def half_of(ref, k, h):
        c, cols = stage(k)
        return ref.at[c, pl.ds(h * half_groups, half_groups), :, cols]

    def remote(src, dst, sems, recvs, where):
        return pltpu.make_async_remote_copy(
            src_ref=src,
            dst_ref=dst,
            send_sem=sems,
            recv_sem=recvs,
            device_id=where,
            device_id_type=MESH,
        )

    locals_ = []
    for k in range(4):
        c, cols = stage(k)

        @pl.loop(1, n_ep)
        def _(i, k=k, c=c, cols=cols):
            peer = lax.rem(ep + i, n_ep)
            remote(
                out_rows.at[c, peer, :, cols],
                mine.at[c, ep, :, cols],
                send_sem.at[k],
                recv_sem.at[k],
                {"ep": peer},
            ).start()

        own = pltpu.make_async_copy(
            out_rows.at[c, ep, :, cols], mine.at[c, ep, :, cols], local_sem.at[k]
        )
        own.start()
        locals_.append(own)

    def all_but_one(ref, k, sem):
        c, cols = stage(k)
        block = ref.at[c, pl.ds(0, n_ep - 1), :, cols]
        return pltpu.make_async_copy(block, block, sem.at[k])

    ring = {}

    def arrive(k):
        locals_[k].wait()
        all_but_one(mine, k, recv_sem).wait()
        plan = [
            (half_of(mine, k, 0), half_of(from_left, k, 0), right),
            (half_of(mine, k, 1), half_of(from_right, k, 1), left),
            (half_of(mine, k, 1), half_of(from_left, k, 1), right),
            (half_of(mine, k, 0), half_of(from_right, k, 0), left),
            (half_of(from_left, k, 0), half_of(from_far, k, 0), right),
            (half_of(from_right, k, 1), half_of(from_far, k, 1), left),
        ]
        ring[k] = [
            remote(src, dst, ring_send.at[k, j], ring_recv.at[k, j], {"half": where})
            for j, (src, dst, where) in enumerate(plan)
        ]
        for j in range(4):
            ring[k][j].start()

    def forward(k):
        ring[k][0].wait_recv()
        ring[k][4].start()
        ring[k][1].wait_recv()
        ring[k][5].start()

    def add(ref, k, h, owner, first=False):
        c, cols = stage(k)
        rows = ref[c, h * half_groups : (h + 1) * half_groups, :, k % 2 * width : (k % 2 + 1) * width]
        at = pl.multiple_of(owner * quarter + k % 2 * width, width)
        term = jnp.dot(
            rows.reshape(half_rows, width), w_in[pl.ds(at, width), :], preferred_element_type=F32
        )
        if first:
            acc[c, h] = term
        else:
            acc[c, h] += term

    def own(k):
        for h in range(2):
            add(mine, k, h, x, first=k % 2 == 0)

    def sides(k):
        add(from_left, k, 0, left)
        add(from_right, k, 1, right)
        ring[k][2].wait_recv()
        add(from_left, k, 1, left)
        ring[k][3].wait_recv()
        add(from_right, k, 0, right)

    def opposite(k):
        ring[k][4].wait_recv()
        add(from_far, k, 0, far)
        ring[k][5].wait_recv()
        add(from_far, k, 1, far)

    def activate(c):
        for h in range(2):
            gate = acc[c, h, :, :ff]
            up = acc[c, h, :, ff:]
            hidden[c, h] = (gate / (1.0 + jnp.exp(-gate)) * up).astype(BF16)

    def down(k, h, owner):
        at = pl.multiple_of(owner * quarter + k % 2 * width, width)
        return jnp.dot(hidden[k // 2, h], w_out[:, pl.ds(at, width)], preferred_element_type=F32)

    sums = {}

    def sum_start(k):
        sums[k] = [
            remote(
                partial.at[k, j],
                inbox.at[k, j],
                sum_send.at[k, j],
                sum_recv.at[k, j],
                {"half": right if j % 2 == 0 else left},
            )
            for j in range(6)
        ]
        for j, (owner, h) in enumerate([(far, 0), (far, 1), (right, 1), (left, 0)]):
            partial[k, j] = down(k, h, owner).astype(BF16)
            sums[k][j].start()

    def sum_middle(k):
        for j, (owner, h) in enumerate([(right, 0), (left, 1)]):
            term = down(k, h, owner)
            sums[k][j].wait_recv()
            partial[k, 4 + j] = (term + inbox[k, j].astype(F32)).astype(BF16)
            sums[k][4 + j].start()

    backs = {}

    def sum_end(k):
        c, cols = stage(k)
        for h, direct, through in ((0, 3, 4), (1, 2, 5)):
            term = down(k, h, x)
            sums[k][direct].wait_recv()
            term = term + inbox[k, direct].astype(F32)
            sums[k][through].wait_recv()
            term = (term + inbox[k, through].astype(F32)).astype(BF16)
            done[
                c,
                h * half_groups : (h + 1) * half_groups,
                :,
                k % 2 * width : (k % 2 + 1) * width,
            ] = term.reshape(half_groups, slots, width)

        @pl.loop(1, n_ep)
        def _(i):
            peer = lax.rem(ep + i, n_ep)
            remote(
                done.at[c, peer, :, cols],
                returned.at[c, ep, :, cols],
                back_send.at[k],
                back_recv.at[k],
                {"ep": peer},
            ).start()

        backs[k] = pltpu.make_async_copy(
            done.at[c, ep, :, cols], returned.at[c, ep, :, cols], back_local.at[k]
        )
        backs[k].start()

    def weigh(k):
        backs[k].wait()
        all_but_one(returned, k, back_recv).wait()
        c = k // 2
        rows = returned[c, :, :, k % 2 * width : (k % 2 + 1) * width].reshape(n_ep * slots, width)
        at = c * n_ep * slots
        gates = combine[:, :, at : at + n_ep * slots].reshape(2 * tokens, n_ep * slots)
        both = jnp.dot(gates, rows, preferred_element_type=F32)
        return both[:tokens] + both[tokens:]

    mixes = []

    def exchange(f, total):
        piece[f] = total.astype(BF16)
        for j, where in enumerate((right, left, far)):
            copy = remote(
                piece.at[f],
                gathered.at[f, j],
                mix_send.at[f, j],
                mix_recv.at[f, j],
                {"half": where},
            )
            copy.start()
            mixes.append(copy)

    arrive(0)
    for load in loads[:2]:
        load.wait()
    own(0)
    forward(0)
    arrive(1)
    sides(0)
    own(1)
    forward(1)
    opposite(0)
    arrive(2)
    sides(1)
    own(2)
    arrive(3)
    opposite(1)
    activate(0)
    loads[2].wait()
    sum_start(0)
    forward(2)
    own(3)
    sum_start(1)
    sum_middle(0)
    forward(3)
    sides(2)
    opposite(2)
    sum_middle(1)
    sum_end(0)
    sides(3)
    opposite(3)
    activate(1)
    sum_start(2)
    sum_end(1)
    sum_start(3)
    sum_middle(2)
    sum_middle(3)
    first = [weigh(0), weigh(1)]
    sum_end(2)
    sum_end(3)
    exchange(0, first[0] + weigh(2))
    exchange(1, first[1] + weigh(3))
    for copy in mixes:
        copy.wait_recv()
    for f in range(2):
        cols = slice(f * width, (f + 1) * width)
        result[x, :, cols] = piece[f]
        for j, owner in enumerate((left, right, far)):
            result[owner, :, cols] = gathered[f, j]
    for k in range(4):
        all_but_one(mine, k, send_sem).wait()
        all_but_one(mine, k, back_send).wait()
        for j in range(6):
            ring[k][j].wait_send()
            sums[k][j].wait_send()
    for copy in mixes:
        copy.wait_send()


def experts(out_rows, combine, w_gate, w_up, w_down):
    chunks, n_ep, slots, quarter = out_rows.shape
    model, ff = w_gate.shape
    tokens = combine.shape[1]
    width = quarter // 2
    half_rows = n_ep // 2 * slots
    rows = pltpu.VMEM((chunks, n_ep, slots, quarter), BF16)
    dma = pltpu.SemaphoreType.DMA
    vmem = pl.BlockSpec(memory_space=pltpu.VMEM)
    hbm = pl.BlockSpec(memory_space=pl.ANY)
    return pl.pallas_call(
        moe_kernel,
        out_shape=jax.ShapeDtypeStruct((4, tokens, quarter), BF16),
        in_specs=[vmem, vmem, hbm, hbm, hbm],
        out_specs=vmem,
        scratch_shapes=[
            pltpu.VMEM((model, 2 * ff), BF16),
            pltpu.VMEM((ff, model), BF16),
            rows,
            rows,
            rows,
            rows,
            pltpu.VMEM((chunks, 2, half_rows, 2 * ff), F32),
            pltpu.VMEM((chunks, 2, half_rows, ff), BF16),
            pltpu.VMEM((4, 6, half_rows, width), BF16),
            pltpu.VMEM((4, 6, half_rows, width), BF16),
            rows,
            rows,
            pltpu.VMEM((2, tokens, width), BF16),
            pltpu.VMEM((2, 3, tokens, width), BF16),
            dma((3,)),
            dma((4,)),
            dma((4,)),
            dma((4,)),
            dma((4, 6)),
            dma((4, 6)),
            dma((4, 6)),
            dma((4, 6)),
            dma((4,)),
            dma((4,)),
            dma((4,)),
            dma((2, 3)),
            dma((2, 3)),
        ],
        compiler_params=pltpu.CompilerParams(
            collective_id=0, has_side_effects=True, vmem_limit_bytes=56 * 2**20
        ),
        cost_estimate=pl.CostEstimate(
            flops=6 * chunks * n_ep * slots * model * ff,
            bytes_accessed=6 * model * ff + 500 * 2**20,
            transcendentals=chunks * n_ep * slots * ff,
        ),
        name="experts",
    )(out_rows, combine, w_gate, w_up, w_down)


def attend(block, prompt_lengths, query, fresh_key, fresh_value):
    group_tok = block.shape[0]
    group_rows = query.shape[0]
    position = jnp.arange(group_tok, dtype=jnp.int32)
    segment = (position >= prompt_lengths[0]).astype(jnp.int32)
    prompt = jnp.arange(group_rows, dtype=jnp.int32) // SAMPLES
    allowed = segment[None, :] == prompt[:, None]
    keys = block[:, :, 0, :]
    values = block[:, :, 1, :]
    scale = 1.0 / math.sqrt(HEAD)
    scores = jnp.einsum("rhgd,thd->rhgt", query, keys, preferred_element_type=F32) * scale
    scores = jnp.where(allowed[:, None, None, :], scores, -1e30)
    own = jnp.einsum("rhgd,rhd->rhg", query, fresh_key, preferred_element_type=F32) * scale
    top = jnp.maximum(jnp.max(scores, axis=3), own)
    spread = jnp.where(allowed[:, None, None, :], jnp.exp(scores - top[..., None]), 0.0)
    self_weight = jnp.exp(own - top)
    total = jnp.sum(spread, axis=3) + self_weight
    probs = (spread / total[..., None]).astype(BF16)
    self_prob = (self_weight / total).astype(BF16)
    mixed = jnp.einsum("rhgt,thd->rhgd", probs, values, preferred_element_type=F32)
    mixed = mixed + self_prob.astype(F32)[..., None] * fresh_value.astype(F32)[:, :, None, :]
    return mixed.astype(BF16).reshape(group_rows, -1)


def route(inputs, chosen, router, n_ep):
    count, top = chosen.shape
    pairs = count * top
    logits = jnp.dot(inputs, router, preferred_element_type=F32)
    onehot = chosen[:, :, None] == jnp.arange(n_ep, dtype=jnp.int32)
    picked = jnp.sum(jnp.where(onehot, logits[:, None, :], 0.0), axis=2)
    weights = jax.nn.softmax(picked, axis=1)
    flags = onehot.reshape(pairs, n_ep).astype(BF16)
    earlier = jnp.tri(pairs, pairs, -1, dtype=BF16)
    before = jnp.dot(earlier, flags, preferred_element_type=F32)
    rank = jnp.sum(before * flags.astype(F32), axis=1).astype(jnp.int32).reshape(count, top)
    slot = rank // SLOTS * (n_ep * SLOTS) + chosen * SLOTS + rank % SLOTS
    select = slot[:, :, None] == jnp.arange(n_ep * CAP, dtype=jnp.int32)
    combine = jnp.sum(jnp.where(select, weights[:, :, None], 0.0), axis=1)
    coarse = combine.astype(BF16)
    fine = (combine - coarse.astype(F32)).astype(BF16)
    return jnp.any(select, axis=1).astype(BF16), jnp.stack([coarse, fine])


def on_device(
    tokens,
    routes,
    router,
    w_gate,
    w_up,
    w_down,
    norm_gain,
    w_kv,
    lengths,
    queries,
    new_keys,
    new_values,
    w_out,
):
    inputs = tokens[0]
    n_ep = lax.axis_size("ep")
    quarter = inputs.shape[1] // lax.axis_size("half")
    select, combine = route(inputs, routes[0], router, n_ep)
    part = lax.dynamic_slice_in_dim(inputs, lax.axis_index("half") * quarter, quarter, 1)
    outgoing = jnp.einsum("ts,td->sd", select, part, preferred_element_type=F32).astype(BF16)
    outgoing = outgoing.reshape(CAP // SLOTS, n_ep, SLOTS, quarter)
    moe = experts(outgoing, combine, w_gate[0], w_up[0], w_down[0])
    moe = moe.transpose(1, 0, 2).reshape(inputs.shape)
    mixed = inputs.astype(F32) + moe.astype(F32)
    meansq = jnp.mean(mixed * mixed, axis=1, keepdims=True)
    normed = (mixed * lax.rsqrt(meansq + 1e-06) * norm_gain).astype(BF16)
    keyvals = jnp.dot(
        normed, lax.all_gather(w_kv, "ep", axis=0, tiled=True), preferred_element_type=F32
    ).astype(BF16)
    remote = lax.ppermute(keyvals, "pool", [(0, 1), (1, 0)])
    other = 1 - lax.axis_index("pool")
    prompt_lengths = lax.dynamic_index_in_dim(lengths, other, 0, keepdims=False)[0]
    kv_heads = new_keys.shape[2] // HEAD
    block = remote.reshape(remote.shape[0], kv_heads, 2, HEAD)
    query = queries[0].reshape(queries.shape[1], kv_heads, -1, HEAD)
    fresh_key = new_keys[0].reshape(new_keys.shape[1], kv_heads, HEAD)
    fresh_value = new_values[0].reshape(new_values.shape[1], kv_heads, HEAD)
    attention = attend(block, prompt_lengths, query, fresh_key, fresh_value)
    decoded = lax.psum_scatter(
        jnp.dot(attention, w_out, preferred_element_type=F32).astype(BF16),
        "half",
        scatter_dimension=0,
        tiled=True,
    )
    return decoded[None]


def solution(mesh):
    in_specs = (
        P("pool", "ep", None),
        P("pool", "ep", None),
        P(),
        P("ep", None, "half"),
        P("ep", None, "half"),
        P("ep", "half", None),
        P(),
        P("ep", "half"),
        P(None, "ep", None),
        P("pool", "ep", "half"),
        P("pool", "ep", "half"),
        P("pool", "ep", "half"),
        P("half", None),
    )
    out_specs = P("pool", ("ep", "half"), None)
    return jax.shard_map(
        on_device, mesh=mesh, in_specs=in_specs, out_specs=out_specs, check_vma=False
    )
```

```python
import math

import jax
import jax.numpy as jnp
from jax import lax
from jax.experimental import pallas as pl
from jax.experimental.pallas import tpu as pltpu
from jax.sharding import PartitionSpec as P

HEAD = 128
SAMPLES = 128
CAP = 32
SLOTS = 16
RING = 8
MESH = pl.DeviceIdType.MESH
BF16 = jnp.bfloat16
F32 = jnp.float32


def moe_kernel(
    tok,
    select,
    gates,
    w_gate,
    w_up,
    w_down,
    result,
    w_in,
    w_out,
    held,
    chosen,
    weights,
    picked,
    mine,
    direct,
    from_left,
    from_right,
    from_far,
    acc,
    hidden,
    partial,
    inbox,
    done,
    returned,
    blend,
    landed,
    piece,
    gathered,
    w_sem,
    tok_sem,
    zring_send,
    zring_recv,
    ctl_local,
    ctl_send,
    ctl_recv,
    y_local,
    y_send,
    y_recv,
    ring_send,
    ring_recv,
    sum_send,
    sum_recv,
    back_local,
    back_send,
    back_recv,
    down_local,
    down_send,
    down_recv,
    mix_send,
    mix_recv,
):
    tokens, columns = tok.shape
    xw = from_left.shape[3]
    dw = columns - xw
    width = xw // 2
    ff = w_gate.shape[1]
    n_ep = mine.shape[1]
    n_z = held.shape[0]
    n_y = n_ep // n_z
    half_groups = n_ep // 2
    half_rows = half_groups * SLOTS
    stripes = partial.shape[1]
    stripe = xw // stripes
    lanes = 2 * n_y * SLOTS
    ep = lax.axis_index("ep")
    y = ep // n_z
    z = lax.rem(ep, n_z)
    x = lax.axis_index("half")
    right = lax.rem(x + 1, 4)
    left = lax.rem(x + 3, 4)
    far = lax.rem(x + 2, 4)

    def at_z(i):
        return {"ep": y * n_z + lax.rem(z + i, n_z)}

    def at_y(i):
        return {"ep": lax.rem(y + i, n_y) * n_z + z}

    loads = [
        pltpu.make_async_copy(w_gate, w_in.at[:, pl.ds(0, ff)], w_sem.at[0]),
        pltpu.make_async_copy(w_up, w_in.at[:, pl.ds(ff, ff)], w_sem.at[1]),
        pltpu.make_async_copy(w_down, w_out, w_sem.at[2]),
    ]
    for load in loads:
        load.start()
    keep = pltpu.make_async_copy(tok, held.at[z], tok_sem)
    keep.start()

    barrier = pltpu.get_barrier_semaphore()

    def greet(where):
        pl.semaphore_signal(barrier, inc=1, device_id=where, device_id_type=MESH)

    @pl.loop(1, n_z)
    def _(i):
        greet(at_z(i))

    @pl.loop(1, n_y)
    def _(i):
        greet(at_y(i))

    for peer in (left, right, far):
        greet({"half": peer})
    pl.semaphore_wait(barrier, n_z + n_y + 1)

    def remote(src, dst, sems, recvs, where):
        return pltpu.make_async_remote_copy(
            src_ref=src,
            dst_ref=dst,
            send_sem=sems,
            recv_sem=recvs,
            device_id=where,
            device_id_type=MESH,
        )

    def wait_for(block, sem):
        pltpu.make_async_copy(block, block, sem).wait()

    parts = [(0, width), (width, width), (xw, dw // 2), (xw + dw // 2, dw // 2)]
    plus = n_z // 2
    minus = n_z - 1 - plus

    def round_copy(p, way, step):
        start, size = parts[p]
        cols = pl.ds(start, size)
        back = n_z - step if way == 0 else step
        block = lax.rem(z + back, n_z)
        src = tok.at[:, cols] if step == 0 else held.at[block, :, cols]
        return remote(
            src,
            held.at[block, :, cols],
            zring_send.at[p, way, step],
            zring_recv.at[p, way, step],
            at_z(1 if way == 0 else n_z - 1),
        )

    trips = {}

    def round_step(p, step):
        for way, steps in ((0, plus), (1, minus)):
            if 0 < step <= steps:
                trips[p, way, step - 1].wait_recv()
            if step < steps:
                trips[p, way, step] = round_copy(p, way, step)
                trips[p, way, step].start()

    def push_control(n, src, dst):
        @pl.loop(1, n_z)
        def _(i):
            there = pl.multiple_of(lax.rem(z + i, n_z) * lanes, lanes)
            remote(
                src.at[:, :, pl.ds(there, lanes)], dst.at[z], ctl_send.at[n], ctl_recv.at[n], at_z(i)
            ).start()

        here = pl.multiple_of(z * lanes, lanes)
        own = pltpu.make_async_copy(src.at[:, :, pl.ds(here, lanes)], dst.at[z], ctl_local.at[n])
        own.start()
        return own

    def wait_control(n, own, dst):
        own.wait()
        wait_for(dst.at[pl.ds(0, n_z - 1)], ctl_recv.at[n])

    def pick(start, size):
        @pl.loop(0, n_z)
        def _(s):
            rows = lax.dot_general(
                chosen[s, 0],
                held[s, :, start : start + size],
                (((0,), (0,)), ((), ())),
                preferred_element_type=F32,
            ).astype(BF16)
            rows = rows.reshape(2 * n_y, SLOTS, size)
            for b in range(2 * n_y):
                picked[b // n_y, b % n_y, s, :, start : start + size] = rows[b]

    y_own = {}

    def push_y(n, c, start, size, dst, dst_start):
        cols = pl.ds(start, size)
        there = dst.at[c, pl.ds(y * n_z, n_z), :, pl.ds(dst_start, size)]

        @pl.loop(1, n_y)
        def _(i):
            peer = lax.rem(y + i, n_y)
            remote(
                picked.at[c, peer, :, :, cols], there, y_send.at[n], y_recv.at[n], at_y(i)
            ).start()

        y_own[n] = pltpu.make_async_copy(picked.at[c, y, :, :, cols], there, y_local.at[n])
        y_own[n].start()

    def others(ref, c, start, size):
        return ref.at[c, pl.ds(0, n_ep - n_z), :, pl.ds(start, size)]

    def stage(k):
        return k // 2, pl.ds(k % 2 * width, width)

    def half_of(ref, k, h):
        c, cols = stage(k)
        return ref.at[c, pl.ds(h * half_groups, half_groups), :, cols]

    ring = {}

    def arrive(k):
        y_own[k].wait()
        wait_for(others(mine, k // 2, k % 2 * width, width), y_recv.at[k])
        plan = [
            (half_of(mine, k, 0), half_of(from_left, k, 0), right),
            (half_of(mine, k, 1), half_of(from_right, k, 1), left),
            (half_of(mine, k, 1), half_of(from_left, k, 1), right),
            (half_of(mine, k, 0), half_of(from_right, k, 0), left),
            (half_of(from_left, k, 0), half_of(from_far, k, 0), right),
            (half_of(from_right, k, 1), half_of(from_far, k, 1), left),
        ]
        ring[k] = [
            remote(src, dst, ring_send.at[k, j], ring_recv.at[k, j], {"half": where})
            for j, (src, dst, where) in enumerate(plan)
        ]
        for j in range(4):
            ring[k][j].start()

    def forward(k):
        ring[k][0].wait_recv()
        ring[k][4].start()
        ring[k][1].wait_recv()
        ring[k][5].start()

    def accumulate(ref, c, h, start, size, at, first=False):
        rows = ref[c, h * half_groups : (h + 1) * half_groups, :, start : start + size]
        term = jnp.dot(
            rows.reshape(half_rows, size), w_in[pl.ds(at, size), :], preferred_element_type=F32
        )
        if first:
            acc[c, h] = term
        else:
            acc[c, h] += term

    def add(ref, k, h, owner, first=False):
        at = pl.multiple_of(owner * xw + k % 2 * width, 128)
        accumulate(ref, k // 2, h, k % 2 * width, width, at, first)

    def own(k):
        for h in range(2):
            add(mine, k, h, x, first=k % 2 == 0)

    def sides(k):
        add(from_left, k, 0, left)
        add(from_right, k, 1, right)
        ring[k][2].wait_recv()
        add(from_left, k, 1, left)
        ring[k][3].wait_recv()
        add(from_right, k, 0, right)

    def opposite(k):
        ring[k][4].wait_recv()
        add(from_far, k, 0, far)
        ring[k][5].wait_recv()
        add(from_far, k, 1, far)

    def straight(c):
        y_own[4 + c].wait()
        wait_for(others(direct, c, 0, dw), y_recv.at[4 + c])
        for h in range(2):
            accumulate(direct, c, h, 0, dw, 4 * xw)

    def activate(c):
        for h in range(2):
            gate = acc[c, h, :, :ff]
            up = acc[c, h, :, ff:]
            hidden[c, h] = (gate / (1.0 + jnp.exp(-gate)) * up).astype(BF16)

    def down(c, s, h, owner):
        at = pl.multiple_of(owner * xw + s * stripe, 128)
        return jnp.dot(hidden[c, h], w_out[:, pl.ds(at, stripe)], preferred_element_type=F32)

    sums = {}

    def sum_start(c, s):
        sums[c, s] = [
            remote(
                partial.at[c, s, j],
                inbox.at[c, s, j],
                sum_send.at[c, s, j],
                sum_recv.at[c, s, j],
                {"half": right if j % 2 == 0 else left},
            )
            for j in range(6)
        ]
        for j, (owner, h) in enumerate([(far, 0), (far, 1), (right, 1), (left, 0)]):
            partial[c, s, j] = down(c, s, h, owner).astype(BF16)
            sums[c, s][j].start()

    def sum_middle(c, s):
        for j, (owner, h) in enumerate([(right, 0), (left, 1)]):
            term = down(c, s, h, owner)
            sums[c, s][j].wait_recv()
            partial[c, s, 4 + j] = (term + inbox[c, s, j].astype(F32)).astype(BF16)
            sums[c, s][4 + j].start()

    backs = {}

    def push_back(n, c, start, size):
        cols = pl.ds(start, size)
        there = returned.at[c, pl.ds(y * n_z, n_z), :, cols]

        @pl.loop(1, n_y)
        def _(i):
            peer = lax.rem(y + i, n_y)
            remote(
                done.at[c, pl.ds(peer * n_z, n_z), :, cols],
                there,
                back_send.at[n, c],
                back_recv.at[n, c],
                at_y(i),
            ).start()

        backs[n, c] = pltpu.make_async_copy(
            done.at[c, pl.ds(y * n_z, n_z), :, cols], there, back_local.at[n, c]
        )
        backs[n, c].start()

    def keep_done(c, h, start, size, term):
        done[c, h * half_groups : (h + 1) * half_groups, :, start : start + size] = term.astype(
            BF16
        ).reshape(half_groups, SLOTS, size)

    def sum_end(c, s):
        for h, near, through in ((0, 3, 4), (1, 2, 5)):
            term = down(c, s, h, x)
            sums[c, s][near].wait_recv()
            term = term + inbox[c, s, near].astype(F32)
            sums[c, s][through].wait_recv()
            term = term + inbox[c, s, through].astype(F32)
            keep_done(c, h, s * stripe, stripe, term)
        push_back(s, c, s * stripe, stripe)

    def straight_out(c):
        for h in range(2):
            term = jnp.dot(hidden[c, h], w_out[:, 4 * xw :], preferred_element_type=F32)
            keep_done(c, h, xw, dw, term)
        push_back(stripes, c, xw, dw)

    spans = [(s * stripe, stripe) for s in range(stripes)] + [(xw, dw)]
    downs = {}

    def combine(n):
        start, size = spans[n]
        cols = pl.ds(start, size)
        for c in range(2):
            backs[n, c].wait()
            wait_for(others(returned, c, start, size), back_recv.at[n, c])

        @pl.loop(0, n_z)
        def _(s):
            rows = jnp.concatenate(
                [
                    returned[c, q * n_z + s, :, start : start + size]
                    for c in range(2)
                    for q in range(n_y)
                ],
                axis=0,
            )
            both = jnp.dot(
                weights[s].reshape(2 * tokens, lanes), rows, preferred_element_type=F32
            )
            blend[s, :, start : start + size] = (both[:tokens] + both[tokens:]).astype(BF16)

        @pl.loop(1, n_z)
        def _(i):
            peer = lax.rem(z + i, n_z)
            remote(
                blend.at[peer, :, cols],
                landed.at[z, :, cols],
                down_send.at[n],
                down_recv.at[n],
                at_z(i),
            ).start()

        downs[n] = pltpu.make_async_copy(
            blend.at[z, :, cols], landed.at[z, :, cols], down_local.at[n]
        )
        downs[n].start()

    mixes = {}

    def exchange(n):
        start, size = spans[n]
        cols = pl.ds(start, size)
        downs[n].wait()
        wait_for(landed.at[pl.ds(0, n_z - 1), :, cols], down_recv.at[n])
        total = landed[0, :, start : start + size].astype(F32)
        for s in range(1, n_z):
            total = total + landed[s, :, start : start + size].astype(F32)
        piece[:, start : start + size] = total.astype(BF16)
        for j, where in enumerate((right, left, far)):
            mixes[n, j] = remote(
                piece.at[:, cols],
                gathered.at[j, :, cols],
                mix_send.at[n, j],
                mix_recv.at[n, j],
                {"half": where},
            )
            mixes[n, j].start()

    round_step(0, 0)
    own_select = push_control(0, select, chosen)
    round_step(1, 0)
    keep.wait()
    for step in range(1, plus):
        round_step(0, step)
        round_step(1, step)
    round_step(0, plus)
    round_step(2, 0)
    round_step(3, 0)
    wait_control(0, own_select, chosen)
    pick(0, width)
    push_y(0, 0, 0, width, mine, 0)
    round_step(1, plus)
    pick(width, width)
    push_y(1, 0, width, width, mine, width)
    push_y(2, 1, 0, width, mine, 0)
    push_y(3, 1, width, width, mine, width)
    round_step(2, 1)
    round_step(3, 1)
    arrive(0)
    round_step(2, 2)
    round_step(3, 2)
    for load in loads[:2]:
        load.wait()
    own(0)
    forward(0)
    arrive(1)
    for step in range(3, plus + 1):
        round_step(2, step)
        round_step(3, step)
    pick(xw, dw)
    push_y(4, 0, xw, dw, direct, 0)
    push_y(5, 1, xw, dw, direct, 0)
    own_gates = push_control(1, gates, weights)
    sides(0)
    arrive(2)
    own(1)
    forward(1)
    opposite(0)
    arrive(3)
    sides(1)
    own(2)
    opposite(1)
    straight(0)
    activate(0)
    loads[2].wait()
    sum_start(0, 0)
    forward(2)
    own(3)
    sum_start(0, 1)
    sum_middle(0, 0)
    forward(3)
    straight_out(0)
    sides(2)
    opposite(2)
    sum_start(0, 2)
    sum_middle(0, 1)
    sum_end(0, 0)
    straight(1)
    sides(3)
    opposite(3)
    activate(1)
    sum_start(1, 0)
    sum_middle(0, 2)
    straight_out(1)
    sum_start(1, 1)
    sum_end(0, 1)
    sum_middle(1, 0)
    sum_start(1, 2)
    sum_end(0, 2)
    sum_middle(1, 1)
    sum_end(1, 0)
    wait_control(1, own_gates, weights)
    combine(stripes)
    sum_middle(1, 2)
    combine(0)
    sum_end(1, 1)
    exchange(stripes)
    combine(1)
    sum_end(1, 2)
    exchange(0)
    exchange(1)
    combine(2)
    exchange(2)
    for n in range(stripes + 1):
        for j in range(3):
            mixes[n, j].wait_recv()
    result[:, pl.ds(pl.multiple_of(x * xw, 128), xw)] = piece[:, :xw]
    shared = piece[:, xw:].astype(F32)
    for j, owner in enumerate((left, right, far)):
        result[:, pl.ds(pl.multiple_of(owner * xw, 128), xw)] = gathered[j, :, :xw]
        shared = shared + gathered[j, :, xw:].astype(F32)
    result[:, 4 * xw :] = shared.astype(BF16)
    for p in range(4):
        for way, steps in ((0, plus), (1, minus)):
            for step in range(steps):
                trips[p, way, step].wait_send()
    wait_for(chosen.at[pl.ds(0, n_z - 1)], ctl_send.at[0])
    wait_for(weights.at[pl.ds(0, n_z - 1)], ctl_send.at[1])
    for k in range(4):
        wait_for(others(mine, k // 2, k % 2 * width, width), y_send.at[k])
        for j in range(6):
            ring[k][j].wait_send()
    for c in range(2):
        wait_for(others(direct, c, 0, dw), y_send.at[4 + c])
        for n, (start, size) in enumerate(spans):
            wait_for(others(returned, c, start, size), back_send.at[n, c])
        for s in range(stripes):
            for j in range(6):
                sums[c, s][j].wait_send()
    for n, (start, size) in enumerate(spans):
        wait_for(landed.at[pl.ds(0, n_z - 1), :, pl.ds(start, size)], down_send.at[n])
        for j in range(3):
            mixes[n, j].wait_send()


def experts(tok, select, gates, w_gate, w_up, w_down, n_ep, n_z, stripes):
    model, ff = w_gate.shape
    tokens, columns = tok.shape
    xw = (model - columns) // 3
    dw = columns - xw
    n_y = n_ep // n_z
    lanes = 2 * n_y * SLOTS
    half_rows = n_ep // 2 * SLOTS
    dma = pltpu.SemaphoreType.DMA
    vmem = pl.BlockSpec(memory_space=pltpu.VMEM)
    hbm = pl.BlockSpec(memory_space=pl.ANY)

    def space(*shape, dtype=BF16):
        return pltpu.VMEM(shape, dtype)

    return pl.pallas_call(
        moe_kernel,
        out_shape=jax.ShapeDtypeStruct((tokens, model), BF16),
        in_specs=[vmem, vmem, vmem, hbm, hbm, hbm],
        out_specs=vmem,
        scratch_shapes=[
            space(model, 2 * ff),
            space(ff, model),
            space(n_z, tokens, columns),
            space(n_z, 1, tokens, lanes),
            space(n_z, 2, tokens, lanes),
            space(2, n_y, n_z, SLOTS, columns),
            space(2, n_ep, SLOTS, xw),
            space(2, n_ep, SLOTS, dw),
            space(2, n_ep, SLOTS, xw),
            space(2, n_ep, SLOTS, xw),
            space(2, n_ep, SLOTS, xw),
            space(2, 2, half_rows, 2 * ff, dtype=F32),
            space(2, 2, half_rows, ff),
            space(2, stripes, 6, half_rows, xw // stripes),
            space(2, stripes, 6, half_rows, xw // stripes),
            space(2, n_ep, SLOTS, columns),
            space(2, n_ep, SLOTS, columns),
            space(n_z, tokens, columns),
            space(n_z, tokens, columns),
            space(tokens, columns),
            space(3, tokens, columns),
            dma((3,)),
            dma,
            dma((4, 2, n_z // 2)),
            dma((4, 2, n_z // 2)),
            dma((2,)),
            dma((2,)),
            dma((2,)),
            dma((6,)),
            dma((6,)),
            dma((6,)),
            dma((4, 6)),
            dma((4, 6)),
            dma((2, stripes, 6)),
            dma((2, stripes, 6)),
            dma((stripes + 1, 2)),
            dma((stripes + 1, 2)),
            dma((stripes + 1, 2)),
            dma((stripes + 1,)),
            dma((stripes + 1,)),
            dma((stripes + 1,)),
            dma((stripes + 1, 3)),
            dma((stripes + 1, 3)),
        ],
        compiler_params=pltpu.CompilerParams(
            collective_id=0, has_side_effects=True, vmem_limit_bytes=58 * 2**20
        ),
        cost_estimate=pl.CostEstimate(
            flops=12 * n_ep * SLOTS * model * ff,
            bytes_accessed=6 * model * ff + 500 * 2**20,
            transcendentals=2 * n_ep * SLOTS * ff,
        ),
        name="experts",
    )(tok, select, gates, w_gate, w_up, w_down)


def attend(block, prompt_lengths, query, fresh_key, fresh_value):
    group_tok = block.shape[0]
    group_rows = query.shape[0]
    position = jnp.arange(group_tok, dtype=jnp.int32)
    segment = (position >= prompt_lengths[0]).astype(jnp.int32)
    prompt = jnp.arange(group_rows, dtype=jnp.int32) // SAMPLES
    allowed = segment[None, :] == prompt[:, None]
    keys = block[:, :, 0, :]
    values = block[:, :, 1, :]
    scale = 1.0 / math.sqrt(HEAD)
    scores = jnp.einsum("rhgd,thd->rhgt", query, keys, preferred_element_type=F32) * scale
    scores = jnp.where(allowed[:, None, None, :], scores, -1e30)
    own = jnp.einsum("rhgd,rhd->rhg", query, fresh_key, preferred_element_type=F32) * scale
    top = jnp.maximum(jnp.max(scores, axis=3), own)
    spread = jnp.where(allowed[:, None, None, :], jnp.exp(scores - top[..., None]), 0.0)
    self_weight = jnp.exp(own - top)
    total = jnp.sum(spread, axis=3) + self_weight
    probs = (spread / total[..., None]).astype(BF16)
    self_prob = (self_weight / total).astype(BF16)
    mixed = jnp.einsum("rhgt,thd->rhgd", probs, values, preferred_element_type=F32)
    mixed = mixed + self_prob.astype(F32)[..., None] * fresh_value.astype(F32)[:, :, None, :]
    return mixed.astype(BF16).reshape(group_rows, -1)


def route(inputs, chosen, router, n_ep, n_z):
    count, top = chosen.shape
    pairs = count * top
    logits = jnp.dot(inputs, router, preferred_element_type=F32)
    onehot = chosen[:, :, None] == jnp.arange(n_ep, dtype=jnp.int32)
    picked = jnp.sum(jnp.where(onehot, logits[:, None, :], 0.0), axis=2)
    weights = jax.nn.softmax(picked, axis=1)
    flags = onehot.reshape(pairs, n_ep).astype(BF16)
    earlier = jnp.tri(pairs, pairs, -1, dtype=BF16)
    before = jnp.dot(earlier, flags, preferred_element_type=F32)
    rank = jnp.sum(before * flags.astype(F32), axis=1).astype(jnp.int32).reshape(count, top)
    n_y = n_ep // n_z
    place = (rank // SLOTS * n_y + chosen // n_z) * SLOTS + rank % SLOTS
    slot = chosen % n_z * (2 * n_y * SLOTS) + place
    select = slot[:, :, None] == jnp.arange(n_ep * CAP, dtype=jnp.int32)
    combine = jnp.sum(jnp.where(select, weights[:, :, None], 0.0), axis=1)
    coarse = combine.astype(BF16)
    fine = (combine - coarse.astype(F32)).astype(BF16)
    return jnp.any(select, axis=1).astype(BF16)[None], jnp.stack([coarse, fine])


def on_device(
    tokens,
    routes,
    router,
    w_gate,
    w_up,
    w_down,
    norm_gain,
    w_kv,
    lengths,
    queries,
    new_keys,
    new_values,
    w_out,
):
    inputs = tokens[0]
    n_ep = lax.axis_size("ep")
    own = inputs.shape[1] * 3 // 16
    select, gates = route(inputs, routes[0], router, n_ep, RING)
    part = lax.dynamic_slice_in_dim(inputs, lax.axis_index("half") * own, own, 1)
    tok = jnp.concatenate([part, inputs[:, 4 * own :]], axis=1)
    moe = experts(tok, select, gates, w_gate[0], w_up[0], w_down[0], n_ep, RING, 3)
    mixed = inputs.astype(F32) + moe.astype(F32)
    meansq = jnp.mean(mixed * mixed, axis=1, keepdims=True)
    normed = (mixed * lax.rsqrt(meansq + 1e-06) * norm_gain).astype(BF16)
    keyvals = jnp.dot(
        normed, lax.all_gather(w_kv, "ep", axis=0, tiled=True), preferred_element_type=F32
    ).astype(BF16)
    remote = lax.ppermute(keyvals, "pool", [(0, 1), (1, 0)])
    other = 1 - lax.axis_index("pool")
    prompt_lengths = lax.dynamic_index_in_dim(lengths, other, 0, keepdims=False)[0]
    kv_heads = new_keys.shape[2] // HEAD
    block = remote.reshape(remote.shape[0], kv_heads, 2, HEAD)
    query = queries[0].reshape(queries.shape[1], kv_heads, -1, HEAD)
    fresh_key = new_keys[0].reshape(new_keys.shape[1], kv_heads, HEAD)
    fresh_value = new_values[0].reshape(new_values.shape[1], kv_heads, HEAD)
    attention = attend(block, prompt_lengths, query, fresh_key, fresh_value)
    decoded = lax.psum_scatter(
        jnp.dot(attention, w_out, preferred_element_type=F32).astype(BF16),
        "half",
        scatter_dimension=0,
        tiled=True,
    )
    return decoded[None]


def solution(mesh):
    in_specs = (
        P("pool", "ep", None),
        P("pool", "ep", None),
        P(),
        P("ep", None, "half"),
        P("ep", None, "half"),
        P("ep", "half", None),
        P(),
        P("ep", "half"),
        P(None, "ep", None),
        P("pool", "ep", "half"),
        P("pool", "ep", "half"),
        P("pool", "ep", "half"),
        P("half", None),
    )
    out_specs = P("pool", ("ep", "half"), None)
    return jax.shard_map(
        on_device, mesh=mesh, in_specs=in_specs, out_specs=out_specs, check_vma=False
    )
```

```python
import math

import jax
import jax.numpy as jnp
from jax import lax
from jax.experimental import pallas as pl
from jax.experimental.pallas import tpu as pltpu
from jax.sharding import PartitionSpec as P

HEAD = 128
SAMPLES = 128
CAP = 32
SLOTS = 16
RING = 8
MESH = pl.DeviceIdType.MESH
BF16 = jnp.bfloat16
F32 = jnp.float32


def moe_kernel(
    tok,
    select,
    gates,
    w_gate,
    w_up,
    w_down,
    result,
    w_in,
    w_out,
    held,
    chosen,
    weights,
    picked,
    mine,
    direct,
    from_left,
    from_right,
    from_far,
    acc,
    hidden,
    partial,
    inbox,
    done,
    returned,
    blend,
    landed,
    piece,
    gathered,
    w_sem,
    tok_sem,
    zring_send,
    zring_recv,
    ctl_local,
    ctl_send,
    ctl_recv,
    y_local,
    y_send,
    y_recv,
    ring_send,
    ring_recv,
    sum_send,
    sum_recv,
    back_local,
    back_send,
    back_recv,
    down_local,
    down_send,
    down_recv,
    mix_send,
    mix_recv,
):
    tokens, columns = tok.shape
    xw = from_left.shape[3]
    dw = columns - xw
    width = xw // 2
    ff = w_gate.shape[1]
    n_ep = mine.shape[1]
    n_z = held.shape[0]
    n_y = n_ep // n_z
    half_groups = n_ep // 2
    half_rows = half_groups * SLOTS
    stripes = partial.shape[1]
    stripe = xw // stripes
    lanes = 2 * n_y * SLOTS
    ep = lax.axis_index("ep")
    y = ep // n_z
    z = lax.rem(ep, n_z)
    x = lax.axis_index("half")
    right = lax.rem(x + 1, 4)
    left = lax.rem(x + 3, 4)
    far = lax.rem(x + 2, 4)

    def at_z(i):
        return {"ep": y * n_z + lax.rem(z + i, n_z)}

    def at_y(i):
        return {"ep": lax.rem(y + i, n_y) * n_z + z}

    loads = [
        pltpu.make_async_copy(w_gate, w_in.at[:, pl.ds(0, ff)], w_sem.at[0]),
        pltpu.make_async_copy(w_up, w_in.at[:, pl.ds(ff, ff)], w_sem.at[1]),
        pltpu.make_async_copy(w_down, w_out, w_sem.at[2]),
    ]
    for load in loads:
        load.start()
    keep = pltpu.make_async_copy(tok, held.at[z], tok_sem)
    keep.start()

    barrier = pltpu.get_barrier_semaphore()

    def greet(where):
        pl.semaphore_signal(barrier, inc=1, device_id=where, device_id_type=MESH)

    @pl.loop(1, n_z)
    def _(i):
        greet(at_z(i))

    @pl.loop(1, n_y)
    def _(i):
        greet(at_y(i))

    for peer in (left, right, far):
        greet({"half": peer})
    pl.semaphore_wait(barrier, n_z + n_y + 1)

    def remote(src, dst, sems, recvs, where):
        return pltpu.make_async_remote_copy(
            src_ref=src,
            dst_ref=dst,
            send_sem=sems,
            recv_sem=recvs,
            device_id=where,
            device_id_type=MESH,
        )

    def wait_for(block, sem):
        pltpu.make_async_copy(block, block, sem).wait()

    parts = [(0, width), (width, width), (xw, dw // 2), (xw + dw // 2, dw // 2)]
    plus = n_z // 2
    minus = n_z - 1 - plus

    def round_copy(p, way, step):
        start, size = parts[p]
        cols = pl.ds(start, size)
        back = n_z - step if way == 0 else step
        block = lax.rem(z + back, n_z)
        src = tok.at[:, cols] if step == 0 else held.at[block, :, cols]
        return remote(
            src,
            held.at[block, :, cols],
            zring_send.at[p, way, step],
            zring_recv.at[p, way, step],
            at_z(1 if way == 0 else n_z - 1),
        )

    trips = {}

    def round_step(p, step):
        for way, steps in ((0, plus), (1, minus)):
            if 0 < step <= steps:
                trips[p, way, step - 1].wait_recv()
            if step < steps:
                trips[p, way, step] = round_copy(p, way, step)
                trips[p, way, step].start()

    def push_control(n, src, dst):
        @pl.loop(1, n_z)
        def _(i):
            there = pl.multiple_of(lax.rem(z + i, n_z) * lanes, lanes)
            remote(
                src.at[:, :, pl.ds(there, lanes)], dst.at[z], ctl_send.at[n], ctl_recv.at[n], at_z(i)
            ).start()

        here = pl.multiple_of(z * lanes, lanes)
        own = pltpu.make_async_copy(src.at[:, :, pl.ds(here, lanes)], dst.at[z], ctl_local.at[n])
        own.start()
        return own

    def wait_control(n, own, dst):
        own.wait()
        wait_for(dst.at[pl.ds(0, n_z - 1)], ctl_recv.at[n])

    def pick(start, size):
        @pl.loop(0, n_z)
        def _(s):
            rows = lax.dot_general(
                chosen[s, 0],
                held[s, :, start : start + size],
                (((0,), (0,)), ((), ())),
                preferred_element_type=F32,
            ).astype(BF16)
            rows = rows.reshape(2 * n_y, SLOTS, size)
            for b in range(2 * n_y):
                picked[b // n_y, b % n_y, s, :, start : start + size] = rows[b]

    y_own = {}

    def push_y(n, c, start, size, dst, dst_start):
        cols = pl.ds(start, size)
        there = dst.at[c, pl.ds(y * n_z, n_z), :, pl.ds(dst_start, size)]

        @pl.loop(1, n_y)
        def _(i):
            peer = lax.rem(y + i, n_y)
            remote(
                picked.at[c, peer, :, :, cols], there, y_send.at[n], y_recv.at[n], at_y(i)
            ).start()

        y_own[n] = pltpu.make_async_copy(picked.at[c, y, :, :, cols], there, y_local.at[n])
        y_own[n].start()

    def others(ref, c, start, size):
        return ref.at[c, pl.ds(0, n_ep - n_z), :, pl.ds(start, size)]

    def stage(k):
        return k // 2, pl.ds(k % 2 * width, width)

    def half_of(ref, k, h):
        c, cols = stage(k)
        return ref.at[c, pl.ds(h * half_groups, half_groups), :, cols]

    ring = {}

    def arrive(k):
        y_own[k].wait()
        wait_for(others(mine, k // 2, k % 2 * width, width), y_recv.at[k])
        plan = [
            (half_of(mine, k, 0), half_of(from_left, k, 0), right),
            (half_of(mine, k, 1), half_of(from_right, k, 1), left),
            (half_of(mine, k, 1), half_of(from_left, k, 1), right),
            (half_of(mine, k, 0), half_of(from_right, k, 0), left),
            (half_of(from_left, k, 0), half_of(from_far, k, 0), right),
            (half_of(from_right, k, 1), half_of(from_far, k, 1), left),
        ]
        ring[k] = [
            remote(src, dst, ring_send.at[k, j], ring_recv.at[k, j], {"half": where})
            for j, (src, dst, where) in enumerate(plan)
        ]
        for j in range(4):
            ring[k][j].start()

    def forward(k):
        ring[k][0].wait_recv()
        ring[k][4].start()
        ring[k][1].wait_recv()
        ring[k][5].start()

    def accumulate(ref, c, h, start, size, at, first=False):
        rows = ref[c, h * half_groups : (h + 1) * half_groups, :, start : start + size]
        term = jnp.dot(
            rows.reshape(half_rows, size), w_in[pl.ds(at, size), :], preferred_element_type=F32
        )
        if first:
            acc[c, h] = term
        else:
            acc[c, h] += term

    def add(ref, k, h, owner, first=False):
        at = pl.multiple_of(owner * xw + k % 2 * width, 128)
        accumulate(ref, k // 2, h, k % 2 * width, width, at, first)

    def own(k):
        for h in range(2):
            add(mine, k, h, x, first=k % 2 == 0)

    def sides(k):
        add(from_left, k, 0, left)
        add(from_right, k, 1, right)
        ring[k][2].wait_recv()
        add(from_left, k, 1, left)
        ring[k][3].wait_recv()
        add(from_right, k, 0, right)

    def opposite(k):
        ring[k][4].wait_recv()
        add(from_far, k, 0, far)
        ring[k][5].wait_recv()
        add(from_far, k, 1, far)

    def straight(c):
        y_own[4 + c].wait()
        wait_for(others(direct, c, 0, dw), y_recv.at[4 + c])
        for h in range(2):
            accumulate(direct, c, h, 0, dw, 4 * xw)

    def activate(c):
        for h in range(2):
            gate = acc[c, h, :, :ff]
            up = acc[c, h, :, ff:]
            hidden[c, h] = (gate / (1.0 + jnp.exp(-gate)) * up).astype(BF16)

    def down(c, s, h, owner):
        at = pl.multiple_of(owner * xw + s * stripe, 128)
        return jnp.dot(hidden[c, h], w_out[:, pl.ds(at, stripe)], preferred_element_type=F32)

    sums = {}

    def sum_start(c, s):
        sums[c, s] = [
            remote(
                partial.at[c, s, j],
                inbox.at[c, s, j],
                sum_send.at[c, s, j],
                sum_recv.at[c, s, j],
                {"half": right if j % 2 == 0 else left},
            )
            for j in range(6)
        ]
        for j, (owner, h) in enumerate([(far, 0), (far, 1), (right, 1), (left, 0)]):
            partial[c, s, j] = down(c, s, h, owner).astype(BF16)
            sums[c, s][j].start()

    def sum_middle(c, s):
        for j, (owner, h) in enumerate([(right, 0), (left, 1)]):
            term = down(c, s, h, owner)
            sums[c, s][j].wait_recv()
            partial[c, s, 4 + j] = (term + inbox[c, s, j].astype(F32)).astype(BF16)
            sums[c, s][4 + j].start()

    backs = {}

    def push_back(n, c, start, size):
        cols = pl.ds(start, size)
        there = returned.at[c, pl.ds(y * n_z, n_z), :, cols]

        @pl.loop(1, n_y)
        def _(i):
            peer = lax.rem(y + i, n_y)
            remote(
                done.at[c, pl.ds(peer * n_z, n_z), :, cols],
                there,
                back_send.at[n, c],
                back_recv.at[n, c],
                at_y(i),
            ).start()

        backs[n, c] = pltpu.make_async_copy(
            done.at[c, pl.ds(y * n_z, n_z), :, cols], there, back_local.at[n, c]
        )
        backs[n, c].start()

    def keep_done(c, h, start, size, term):
        done[c, h * half_groups : (h + 1) * half_groups, :, start : start + size] = term.astype(
            BF16
        ).reshape(half_groups, SLOTS, size)

    def sum_end(c, s):
        for h, near, through in ((0, 3, 4), (1, 2, 5)):
            term = down(c, s, h, x)
            sums[c, s][near].wait_recv()
            term = term + inbox[c, s, near].astype(F32)
            sums[c, s][through].wait_recv()
            term = term + inbox[c, s, through].astype(F32)
            keep_done(c, h, s * stripe, stripe, term)
        push_back(s, c, s * stripe, stripe)

    def straight_out(c):
        for h in range(2):
            term = jnp.dot(hidden[c, h], w_out[:, 4 * xw :], preferred_element_type=F32)
            keep_done(c, h, xw, dw, term)
        push_back(stripes, c, xw, dw)

    spans = [(s * stripe, stripe) for s in range(stripes)] + [(xw, dw)]
    downs = {}

    def combine(n):
        start, size = spans[n]
        cols = pl.ds(start, size)
        for c in range(2):
            backs[n, c].wait()
            wait_for(others(returned, c, start, size), back_recv.at[n, c])

        @pl.loop(0, n_z)
        def _(s):
            rows = jnp.concatenate(
                [
                    returned[c, q * n_z + s, :, start : start + size]
                    for c in range(2)
                    for q in range(n_y)
                ],
                axis=0,
            )
            both = jnp.dot(
                weights[s].reshape(2 * tokens, lanes), rows, preferred_element_type=F32
            )
            blend[s, :, start : start + size] = (both[:tokens] + both[tokens:]).astype(BF16)

        @pl.loop(1, n_z)
        def _(i):
            peer = lax.rem(z + i, n_z)
            remote(
                blend.at[peer, :, cols],
                landed.at[z, :, cols],
                down_send.at[n],
                down_recv.at[n],
                at_z(i),
            ).start()

        downs[n] = pltpu.make_async_copy(
            blend.at[z, :, cols], landed.at[z, :, cols], down_local.at[n]
        )
        downs[n].start()

    mixes = {}

    def exchange(n):
        start, size = spans[n]
        cols = pl.ds(start, size)
        downs[n].wait()
        wait_for(landed.at[pl.ds(0, n_z - 1), :, cols], down_recv.at[n])
        total = landed[0, :, start : start + size].astype(F32)
        for s in range(1, n_z):
            total = total + landed[s, :, start : start + size].astype(F32)
        piece[:, start : start + size] = total.astype(BF16)
        for j, where in enumerate((right, left, far)):
            mixes[n, j] = remote(
                piece.at[:, cols],
                gathered.at[j, :, cols],
                mix_send.at[n, j],
                mix_recv.at[n, j],
                {"half": where},
            )
            mixes[n, j].start()

    round_step(0, 0)
    own_select = push_control(0, select, chosen)
    round_step(1, 0)
    keep.wait()
    for step in range(1, plus):
        round_step(0, step)
        round_step(1, step)
    round_step(0, plus)
    round_step(2, 0)
    round_step(3, 0)
    wait_control(0, own_select, chosen)
    pick(0, width)
    push_y(0, 0, 0, width, mine, 0)
    round_step(1, plus)
    pick(width, width)
    push_y(1, 0, width, width, mine, width)
    push_y(2, 1, 0, width, mine, 0)
    push_y(3, 1, width, width, mine, width)
    round_step(2, 1)
    round_step(3, 1)
    arrive(0)
    round_step(2, 2)
    round_step(3, 2)
    for load in loads[:2]:
        load.wait()
    own(0)
    forward(0)
    arrive(1)
    for step in range(3, plus + 1):
        round_step(2, step)
        round_step(3, step)
    pick(xw, dw)
    push_y(4, 0, xw, dw, direct, 0)
    push_y(5, 1, xw, dw, direct, 0)
    own_gates = push_control(1, gates, weights)
    sides(0)
    arrive(2)
    own(1)
    forward(1)
    opposite(0)
    arrive(3)
    sides(1)
    own(2)
    opposite(1)
    straight(0)
    activate(0)
    loads[2].wait()
    sum_start(0, 0)
    forward(2)
    own(3)
    sum_start(0, 1)
    sum_middle(0, 0)
    forward(3)
    straight_out(0)
    sides(2)
    opposite(2)
    sum_start(0, 2)
    sum_middle(0, 1)
    sum_end(0, 0)
    straight(1)
    sides(3)
    opposite(3)
    activate(1)
    sum_start(1, 0)
    sum_middle(0, 2)
    straight_out(1)
    sum_start(1, 1)
    sum_end(0, 1)
    sum_middle(1, 0)
    sum_start(1, 2)
    sum_end(0, 2)
    sum_middle(1, 1)
    sum_end(1, 0)
    wait_control(1, own_gates, weights)
    combine(stripes)
    sum_middle(1, 2)
    combine(0)
    sum_end(1, 1)
    exchange(stripes)
    combine(1)
    sum_end(1, 2)
    exchange(0)
    exchange(1)
    combine(2)
    exchange(2)
    for n in range(stripes + 1):
        for j in range(3):
            mixes[n, j].wait_recv()
    result[:, pl.ds(pl.multiple_of(x * xw, 128), xw)] = piece[:, :xw]
    shared = piece[:, xw:].astype(F32)
    for j, owner in enumerate((left, right, far)):
        result[:, pl.ds(pl.multiple_of(owner * xw, 128), xw)] = gathered[j, :, :xw]
        shared = shared + gathered[j, :, xw:].astype(F32)
    result[:, 4 * xw :] = shared.astype(BF16)
    for p in range(4):
        for way, steps in ((0, plus), (1, minus)):
            for step in range(steps):
                trips[p, way, step].wait_send()
    wait_for(chosen.at[pl.ds(0, n_z - 1)], ctl_send.at[0])
    wait_for(weights.at[pl.ds(0, n_z - 1)], ctl_send.at[1])
    for k in range(4):
        wait_for(others(mine, k // 2, k % 2 * width, width), y_send.at[k])
        for j in range(6):
            ring[k][j].wait_send()
    for c in range(2):
        wait_for(others(direct, c, 0, dw), y_send.at[4 + c])
        for n, (start, size) in enumerate(spans):
            wait_for(others(returned, c, start, size), back_send.at[n, c])
        for s in range(stripes):
            for j in range(6):
                sums[c, s][j].wait_send()
    for n, (start, size) in enumerate(spans):
        wait_for(landed.at[pl.ds(0, n_z - 1), :, pl.ds(start, size)], down_send.at[n])
        for j in range(3):
            mixes[n, j].wait_send()


def experts(tok, select, gates, w_gate, w_up, w_down, n_ep, n_z, stripes):
    model, ff = w_gate.shape
    tokens, columns = tok.shape
    xw = (model - columns) // 3
    dw = columns - xw
    n_y = n_ep // n_z
    lanes = 2 * n_y * SLOTS
    half_rows = n_ep // 2 * SLOTS
    dma = pltpu.SemaphoreType.DMA
    vmem = pl.BlockSpec(memory_space=pltpu.VMEM)
    hbm = pl.BlockSpec(memory_space=pl.ANY)

    def space(*shape, dtype=BF16):
        return pltpu.VMEM(shape, dtype)

    return pl.pallas_call(
        moe_kernel,
        out_shape=jax.ShapeDtypeStruct((tokens, model), BF16),
        in_specs=[vmem, vmem, vmem, hbm, hbm, hbm],
        out_specs=vmem,
        scratch_shapes=[
            space(model, 2 * ff),
            space(ff, model),
            space(n_z, tokens, columns),
            space(n_z, 1, tokens, lanes),
            space(n_z, 2, tokens, lanes),
            space(2, n_y, n_z, SLOTS, columns),
            space(2, n_ep, SLOTS, xw),
            space(2, n_ep, SLOTS, dw),
            space(2, n_ep, SLOTS, xw),
            space(2, n_ep, SLOTS, xw),
            space(2, n_ep, SLOTS, xw),
            space(2, 2, half_rows, 2 * ff, dtype=F32),
            space(2, 2, half_rows, ff),
            space(2, stripes, 6, half_rows, xw // stripes),
            space(2, stripes, 6, half_rows, xw // stripes),
            space(2, n_ep, SLOTS, columns),
            space(2, n_ep, SLOTS, columns),
            space(n_z, tokens, columns),
            space(n_z, tokens, columns),
            space(tokens, columns),
            space(3, tokens, columns),
            dma((3,)),
            dma,
            dma((4, 2, n_z // 2)),
            dma((4, 2, n_z // 2)),
            dma((2,)),
            dma((2,)),
            dma((2,)),
            dma((6,)),
            dma((6,)),
            dma((6,)),
            dma((4, 6)),
            dma((4, 6)),
            dma((2, stripes, 6)),
            dma((2, stripes, 6)),
            dma((stripes + 1, 2)),
            dma((stripes + 1, 2)),
            dma((stripes + 1, 2)),
            dma((stripes + 1,)),
            dma((stripes + 1,)),
            dma((stripes + 1,)),
            dma((stripes + 1, 3)),
            dma((stripes + 1, 3)),
        ],
        compiler_params=pltpu.CompilerParams(
            collective_id=0, has_side_effects=True, vmem_limit_bytes=58 * 2**20
        ),
        cost_estimate=pl.CostEstimate(
            flops=12 * n_ep * SLOTS * model * ff,
            bytes_accessed=6 * model * ff + 500 * 2**20,
            transcendentals=2 * n_ep * SLOTS * ff,
        ),
        name="experts",
    )(tok, select, gates, w_gate, w_up, w_down)


def decode_kernel(
    tok,
    moe,
    gain,
    w_kv,
    allowed,
    queries,
    new_keys,
    new_values,
    w_out,
    result,
    w_kv_here,
    w_out_here,
    own_kv,
    other_kv,
    heads,
    partial,
    inbox,
    load_sem,
    swap_send,
    swap_recv,
    send_sem,
    recv_sem,
):
    x = lax.axis_index("half")
    right = lax.rem(x + 1, 4)
    left = lax.rem(x + 3, 4)
    far = lax.rem(x + 2, 4)
    partner = {"pool": 1 - lax.axis_index("pool")}
    load_kv = pltpu.make_async_copy(w_kv, w_kv_here, load_sem.at[0])
    load_out = pltpu.make_async_copy(w_out, w_out_here, load_sem.at[1])
    load_kv.start()
    load_out.start()
    barrier = pltpu.get_barrier_semaphore()
    pl.semaphore_signal(barrier, inc=1, device_id=partner, device_id_type=MESH)
    for peer in (left, right, far):
        pl.semaphore_signal(barrier, inc=1, device_id={"half": peer}, device_id_type=MESH)

    mixed = tok[...].astype(F32) + moe[...].astype(F32)
    meansq = jnp.mean(mixed * mixed, axis=1, keepdims=True)
    normed = (mixed * lax.rsqrt(meansq + 1e-06) * gain[...]).astype(BF16)
    load_kv.wait()
    own_kv[...] = jnp.dot(normed, w_kv_here[...], preferred_element_type=F32).astype(BF16)
    pl.semaphore_wait(barrier, 4)
    swap = pltpu.make_async_remote_copy(
        src_ref=own_kv,
        dst_ref=other_kv,
        send_sem=swap_send,
        recv_sem=swap_recv,
        device_id=partner,
        device_id_type=MESH,
    )
    swap.start()
    rows = queries.shape[0] // 4
    kv_heads = new_keys.shape[1] // HEAD
    shared = queries.shape[1] // new_keys.shape[1]
    scale = 1.0 / math.sqrt(HEAD)
    swap.wait_recv()
    load_out.wait()

    def block(owner):
        at = pl.ds(pl.multiple_of(owner * rows, rows), rows)
        seen = allowed[at, :] > 0.0
        for h in range(kv_heads):
            keys = other_kv[:, 2 * h * HEAD : (2 * h + 1) * HEAD]
            values = other_kv[:, (2 * h + 1) * HEAD : (2 * h + 2) * HEAD]
            fresh_key = new_keys[at, h * HEAD : (h + 1) * HEAD].astype(F32)
            fresh_value = new_values[at, h * HEAD : (h + 1) * HEAD].astype(F32)
            for g in range(shared):
                cols = slice((h * shared + g) * HEAD, (h * shared + g + 1) * HEAD)
                query = queries[at, cols]
                scores = lax.dot_general(
                    query, keys, (((1,), (1,)), ((), ())), preferred_element_type=F32
                )
                scores = jnp.where(seen, scores * scale, -1e30)
                own = jnp.sum(query.astype(F32) * fresh_key, axis=1, keepdims=True) * scale
                top = jnp.maximum(jnp.max(scores, axis=1, keepdims=True), own)
                spread = jnp.where(seen, jnp.exp(scores - top), 0.0)
                self_weight = jnp.exp(own - top)
                total = jnp.sum(spread, axis=1, keepdims=True) + self_weight
                probs = (spread / total).astype(BF16)
                self_prob = (self_weight / total).astype(BF16).astype(F32)
                value = jnp.dot(probs, values, preferred_element_type=F32)
                heads[:, cols] = (value + self_prob * fresh_value).astype(BF16)
        return jnp.dot(heads[...], w_out_here[...], preferred_element_type=F32)

    copies = []
    for j, owner in enumerate((far, right, left)):
        partial[j] = block(owner).astype(BF16)
        copy = pltpu.make_async_remote_copy(
            src_ref=partial.at[j],
            dst_ref=inbox.at[j],
            send_sem=send_sem.at[j],
            recv_sem=recv_sem.at[j],
            device_id={"half": owner},
            device_id_type=MESH,
        )
        copy.start()
        copies.append(copy)
    total = block(x).astype(BF16).astype(F32)
    for j in (1, 2, 0):
        copies[j].wait_recv()
        total = total + inbox[j].astype(F32)
    result[...] = total.astype(BF16)
    swap.wait_send()
    for copy in copies:
        copy.wait_send()


def decode(tok, moe, gain, w_kv, allowed, queries, new_keys, new_values, w_out):
    rows, inner = queries.shape[0] // 4, queries.shape[1]
    wide = w_out.shape[1]
    dma = pltpu.SemaphoreType.DMA
    vmem = pl.BlockSpec(memory_space=pltpu.VMEM)
    hbm = pl.BlockSpec(memory_space=pl.ANY)
    return pl.pallas_call(
        decode_kernel,
        out_shape=jax.ShapeDtypeStruct((rows, wide), BF16),
        in_specs=[vmem, vmem, vmem, hbm, vmem, vmem, vmem, vmem, hbm],
        out_specs=vmem,
        scratch_shapes=[
            pltpu.VMEM(w_kv.shape, BF16),
            pltpu.VMEM(w_out.shape, BF16),
            pltpu.VMEM((tok.shape[0], w_kv.shape[1]), BF16),
            pltpu.VMEM((tok.shape[0], w_kv.shape[1]), BF16),
            pltpu.VMEM((rows, inner), BF16),
            pltpu.VMEM((3, rows, wide), BF16),
            pltpu.VMEM((3, rows, wide), BF16),
            dma((2,)),
            dma,
            dma,
            dma((3,)),
            dma((3,)),
        ],
        compiler_params=pltpu.CompilerParams(
            collective_id=1, has_side_effects=True, vmem_limit_bytes=32 * 2**20
        ),
        cost_estimate=pl.CostEstimate(
            flops=2 * tok.shape[0] * w_kv.size + 8 * rows * w_out.size,
            bytes_accessed=2 * (w_kv.size + w_out.size),
            transcendentals=8 * rows * tok.shape[0] * 8,
        ),
        name="decode",
    )(tok, moe, gain, w_kv, allowed, queries, new_keys, new_values, w_out)


def route(inputs, chosen, router, n_ep, n_z):
    count, top = chosen.shape
    pairs = count * top
    logits = jnp.dot(inputs, router, preferred_element_type=F32)
    onehot = chosen[:, :, None] == jnp.arange(n_ep, dtype=jnp.int32)
    picked = jnp.sum(jnp.where(onehot, logits[:, None, :], 0.0), axis=2)
    weights = jax.nn.softmax(picked, axis=1)
    flags = onehot.reshape(pairs, n_ep).astype(BF16)
    earlier = jnp.tri(pairs, pairs, -1, dtype=BF16)
    before = jnp.dot(earlier, flags, preferred_element_type=F32)
    rank = jnp.sum(before * flags.astype(F32), axis=1).astype(jnp.int32).reshape(count, top)
    n_y = n_ep // n_z
    place = (rank // SLOTS * n_y + chosen // n_z) * SLOTS + rank % SLOTS
    slot = chosen % n_z * (2 * n_y * SLOTS) + place
    select = slot[:, :, None] == jnp.arange(n_ep * CAP, dtype=jnp.int32)
    combine = jnp.sum(jnp.where(select, weights[:, :, None], 0.0), axis=1)
    coarse = combine.astype(BF16)
    fine = (combine - coarse.astype(F32)).astype(BF16)
    return jnp.any(select, axis=1).astype(BF16)[None], jnp.stack([coarse, fine])


def on_device(
    tokens,
    routes,
    router,
    w_gate,
    w_up,
    w_down,
    norm_gain,
    w_kv,
    lengths,
    queries,
    new_keys,
    new_values,
    w_out,
):
    inputs = tokens[0]
    n_ep = lax.axis_size("ep")
    own = inputs.shape[1] * 3 // 16
    select, gates = route(inputs, routes[0], router, n_ep, RING)
    part = lax.dynamic_slice_in_dim(inputs, lax.axis_index("half") * own, own, 1)
    tok = jnp.concatenate([part, inputs[:, 4 * own :]], axis=1)
    moe = experts(tok, select, gates, w_gate[0], w_up[0], w_down[0], n_ep, RING, 3)
    rows = w_kv.shape[0] // 2
    pool = lax.axis_index("pool")
    mine = lax.dynamic_slice_in_dim(w_kv, pool * rows, rows, 0)
    w_all = lax.all_gather(mine, ("ep", "pool"), axis=0, tiled=True)
    first = lax.dynamic_slice(lengths, (1 - pool, 0, 0), (1, 1, 1))[0]
    second = jnp.arange(inputs.shape[0], dtype=jnp.int32)[None, :] >= first
    prompt = jnp.arange(queries.shape[1], dtype=jnp.int32)[:, None] // SAMPLES
    allowed = (second == (prompt == 1)).astype(F32)
    return decode(
        inputs, moe, norm_gain[None], w_all, allowed, queries[0], new_keys[0], new_values[0], w_out
    )[None]


def solution(mesh):
    in_specs = (
        P("pool", "ep", None),
        P("pool", "ep", None),
        P(),
        P("ep", None, "half"),
        P("ep", None, "half"),
        P("ep", "half", None),
        P(),
        P("ep", "half"),
        P(None, "ep", None),
        P("pool", "ep", "half"),
        P("pool", "ep", "half"),
        P("pool", "ep", "half"),
        P("half", None),
    )
    out_specs = P("pool", ("ep", "half"), None)
    return jax.shard_map(
        on_device, mesh=mesh, in_specs=in_specs, out_specs=out_specs, check_vma=False
    )
```

```python
import math

import jax
import jax.numpy as jnp
from jax import lax
from jax.experimental import pallas as pl
from jax.experimental.pallas import tpu as pltpu
from jax.sharding import PartitionSpec as P

HEAD = 128
SAMPLES = 128
CAP = 32
SLOTS = 16
RING = 8
MESH = pl.DeviceIdType.MESH
BF16 = jnp.bfloat16
F32 = jnp.float32


def moe_kernel(
    tok,
    routes,
    router,
    w_gate,
    w_up,
    w_down,
    result,
    router_here,
    select,
    gates,
    w_in,
    w_out,
    held,
    chosen,
    weights,
    picked,
    mine,
    direct,
    from_left,
    from_right,
    from_far,
    acc,
    hidden,
    partial,
    inbox,
    done,
    returned,
    blend,
    landed,
    piece,
    gathered,
    w_sem,
    tok_sem,
    zring_send,
    zring_recv,
    ctl_local,
    ctl_send,
    ctl_recv,
    y_local,
    y_send,
    y_recv,
    ring_send,
    ring_recv,
    sum_send,
    sum_recv,
    back_local,
    back_send,
    back_recv,
    down_local,
    down_send,
    down_recv,
    mix_send,
    mix_recv,
):
    tokens = tok.shape[0]
    columns = held.shape[2]
    xw = from_left.shape[3]
    dw = columns - xw
    width = xw // 2
    ff = w_gate.shape[1]
    n_ep = mine.shape[1]
    n_z = held.shape[0]
    n_y = n_ep // n_z
    half_groups = n_ep // 2
    half_rows = half_groups * SLOTS
    stripes = partial.shape[1]
    stripe = xw // stripes
    lanes = 2 * n_y * SLOTS
    ep = lax.axis_index("ep")
    y = ep // n_z
    z = lax.rem(ep, n_z)
    x = lax.axis_index("half")
    right = lax.rem(x + 1, 4)
    left = lax.rem(x + 3, 4)
    far = lax.rem(x + 2, 4)

    def at_z(i):
        return {"ep": y * n_z + lax.rem(z + i, n_z)}

    def at_y(i):
        return {"ep": lax.rem(y + i, n_y) * n_z + z}

    loads = [
        pltpu.make_async_copy(w_gate, w_in.at[:, pl.ds(0, ff)], w_sem.at[0]),
        pltpu.make_async_copy(w_up, w_in.at[:, pl.ds(ff, ff)], w_sem.at[1]),
        pltpu.make_async_copy(w_down, w_out, w_sem.at[2]),
    ]
    for load in loads:
        load.start()
    load_router = pltpu.make_async_copy(router, router_here, w_sem.at[3])
    load_router.start()
    own_cols = pl.ds(pl.multiple_of(x * xw, 128), xw)
    keeps = [
        pltpu.make_async_copy(tok.at[:, own_cols], held.at[z, :, pl.ds(0, xw)], tok_sem.at[0]),
        pltpu.make_async_copy(
            tok.at[:, pl.ds(4 * xw, dw)], held.at[z, :, pl.ds(xw, dw)], tok_sem.at[1]
        ),
    ]
    for keep in keeps:
        keep.start()

    barrier = pltpu.get_barrier_semaphore()

    def greet(where):
        pl.semaphore_signal(barrier, inc=1, device_id=where, device_id_type=MESH)

    @pl.loop(1, n_z)
    def _(i):
        greet(at_z(i))

    @pl.loop(1, n_y)
    def _(i):
        greet(at_y(i))

    for peer in (left, right, far):
        greet({"half": peer})

    load_router.wait()
    logits = lax.dot_general(
        tok[...], router_here[...], (((1,), (1,)), ((), ())), preferred_element_type=F32
    )
    expert = lax.broadcasted_iota(jnp.int32, (n_ep, tokens), 0)
    naming = jnp.zeros((n_ep, tokens), F32)
    for k in range(routes.shape[0]):
        naming = naming + jnp.where(routes[k : k + 1, :] == expert, 1.0, 0.0)
    row = lax.broadcasted_iota(jnp.int32, (tokens, tokens), 0)
    column = lax.broadcasted_iota(jnp.int32, (tokens, tokens), 1)

    def by_token(pairs):
        return lax.dot_general(
            jnp.where(pairs, 1.0, 0.0).astype(BF16),
            naming.astype(BF16),
            (((1,), (1,)), ((), ())),
            preferred_element_type=F32,
        )

    named = by_token(column == row)
    rank = by_token(column < row)
    top = jnp.max(jnp.where(named > 0.0, logits, -jnp.inf), axis=1, keepdims=True)
    spread = jnp.where(named > 0.0, jnp.exp(jnp.minimum(logits - top, 0.0)), 0.0)
    gate_of = spread / jnp.sum(spread, axis=1, keepdims=True)
    coarse = gate_of.astype(BF16)
    fine = (gate_of - coarse.astype(F32)).astype(BF16)

    def bits(value, size):
        return lax.shift_right_logical(value, jnp.int32(size.bit_length() - 1))

    def slot_facts(count):
        lane = lax.broadcasted_iota(jnp.int32, (count, n_ep * CAP), 1)
        inner = lane & (lanes - 1)
        whose = (bits(inner, SLOTS) & (n_y - 1)) * n_z + bits(lane, lanes)
        return whose, bits(inner, n_y * SLOTS) * SLOTS + (inner & (SLOTS - 1))

    whose, _ = slot_facts(n_ep)
    spreader = jnp.where(
        whose == lax.broadcasted_iota(jnp.int32, whose.shape, 0), 1.0, 0.0
    ).astype(BF16)

    def to_slots(table):
        return jnp.dot(table.astype(BF16), spreader, preferred_element_type=F32)

    _, place = slot_facts(tokens)
    held_here = (to_slots(named) > 0.0) & (to_slots(rank) == place.astype(F32))
    select[0] = jnp.where(held_here, 1.0, 0.0).astype(BF16)
    gates[0] = jnp.where(held_here, to_slots(coarse), 0.0).astype(BF16)
    gates[1] = jnp.where(held_here, to_slots(fine), 0.0).astype(BF16)
    pl.semaphore_wait(barrier, n_z + n_y + 1)

    def remote(src, dst, sems, recvs, where):
        return pltpu.make_async_remote_copy(
            src_ref=src,
            dst_ref=dst,
            send_sem=sems,
            recv_sem=recvs,
            device_id=where,
            device_id_type=MESH,
        )

    def wait_for(block, sem):
        pltpu.make_async_copy(block, block, sem).wait()

    parts = [(0, width), (width, width), (xw, dw // 2), (xw + dw // 2, dw // 2)]
    plus = n_z // 2
    minus = n_z - 1 - plus

    def round_copy(p, way, step):
        start, size = parts[p]
        cols = pl.ds(start, size)
        back = n_z - step if way == 0 else step
        block = lax.rem(z + back, n_z)
        if step == 0:
            base = x * xw + start if start < xw else 3 * xw + start
            src = tok.at[:, pl.ds(pl.multiple_of(base, 128), size)]
        else:
            src = held.at[block, :, cols]
        return remote(
            src,
            held.at[block, :, cols],
            zring_send.at[p, way, step],
            zring_recv.at[p, way, step],
            at_z(1 if way == 0 else n_z - 1),
        )

    trips = {}

    def round_step(p, step):
        for way, steps in ((0, plus), (1, minus)):
            if 0 < step <= steps:
                trips[p, way, step - 1].wait_recv()
            if step < steps:
                trips[p, way, step] = round_copy(p, way, step)
                trips[p, way, step].start()

    def push_control(n, src, dst):
        @pl.loop(1, n_z)
        def _(i):
            there = pl.multiple_of(lax.rem(z + i, n_z) * lanes, lanes)
            remote(
                src.at[:, :, pl.ds(there, lanes)], dst.at[z], ctl_send.at[n], ctl_recv.at[n], at_z(i)
            ).start()

        here = pl.multiple_of(z * lanes, lanes)
        own = pltpu.make_async_copy(src.at[:, :, pl.ds(here, lanes)], dst.at[z], ctl_local.at[n])
        own.start()
        return own

    def wait_control(n, own, dst):
        own.wait()
        wait_for(dst.at[pl.ds(0, n_z - 1)], ctl_recv.at[n])

    def pick(start, size):
        @pl.loop(0, n_z)
        def _(s):
            rows = lax.dot_general(
                chosen[s, 0],
                held[s, :, start : start + size],
                (((0,), (0,)), ((), ())),
                preferred_element_type=F32,
            ).astype(BF16)
            rows = rows.reshape(2 * n_y, SLOTS, size)
            for b in range(2 * n_y):
                picked[b // n_y, b % n_y, s, :, start : start + size] = rows[b]

    y_own = {}

    def push_y(n, c, start, size, dst, dst_start):
        cols = pl.ds(start, size)
        there = dst.at[c, pl.ds(y * n_z, n_z), :, pl.ds(dst_start, size)]

        @pl.loop(1, n_y)
        def _(i):
            peer = lax.rem(y + i, n_y)
            remote(
                picked.at[c, peer, :, :, cols], there, y_send.at[n], y_recv.at[n], at_y(i)
            ).start()

        y_own[n] = pltpu.make_async_copy(picked.at[c, y, :, :, cols], there, y_local.at[n])
        y_own[n].start()

    def others(ref, c, start, size):
        return ref.at[c, pl.ds(0, n_ep - n_z), :, pl.ds(start, size)]

    def stage(k):
        return k // 2, pl.ds(k % 2 * width, width)

    def half_of(ref, k, h):
        c, cols = stage(k)
        return ref.at[c, pl.ds(h * half_groups, half_groups), :, cols]

    ring = {}

    def arrive(k):
        y_own[k].wait()
        wait_for(others(mine, k // 2, k % 2 * width, width), y_recv.at[k])
        plan = [
            (half_of(mine, k, 0), half_of(from_left, k, 0), right),
            (half_of(mine, k, 1), half_of(from_right, k, 1), left),
            (half_of(mine, k, 1), half_of(from_left, k, 1), right),
            (half_of(mine, k, 0), half_of(from_right, k, 0), left),
            (half_of(from_left, k, 0), half_of(from_far, k, 0), right),
            (half_of(from_right, k, 1), half_of(from_far, k, 1), left),
        ]
        ring[k] = [
            remote(src, dst, ring_send.at[k, j], ring_recv.at[k, j], {"half": where})
            for j, (src, dst, where) in enumerate(plan)
        ]
        for j in range(4):
            ring[k][j].start()

    def forward(k):
        ring[k][0].wait_recv()
        ring[k][4].start()
        ring[k][1].wait_recv()
        ring[k][5].start()

    def accumulate(ref, c, h, start, size, at, first=False):
        rows = ref[c, h * half_groups : (h + 1) * half_groups, :, start : start + size]
        term = jnp.dot(
            rows.reshape(half_rows, size), w_in[pl.ds(at, size), :], preferred_element_type=F32
        )
        if first:
            acc[c, h] = term
        else:
            acc[c, h] += term

    def add(ref, k, h, owner, first=False):
        at = pl.multiple_of(owner * xw + k % 2 * width, 128)
        accumulate(ref, k // 2, h, k % 2 * width, width, at, first)

    def own(k):
        for h in range(2):
            add(mine, k, h, x, first=k % 2 == 0)

    def sides(k):
        add(from_left, k, 0, left)
        add(from_right, k, 1, right)
        ring[k][2].wait_recv()
        add(from_left, k, 1, left)
        ring[k][3].wait_recv()
        add(from_right, k, 0, right)

    def opposite(k):
        ring[k][4].wait_recv()
        add(from_far, k, 0, far)
        ring[k][5].wait_recv()
        add(from_far, k, 1, far)

    def straight(c):
        y_own[4 + c].wait()
        wait_for(others(direct, c, 0, dw), y_recv.at[4 + c])
        for h in range(2):
            accumulate(direct, c, h, 0, dw, 4 * xw)

    def activate(c):
        for h in range(2):
            gate = acc[c, h, :, :ff]
            up = acc[c, h, :, ff:]
            hidden[c, h] = (gate / (1.0 + jnp.exp(-gate)) * up).astype(BF16)

    def down(c, s, h, owner):
        at = pl.multiple_of(owner * xw + s * stripe, 128)
        return jnp.dot(hidden[c, h], w_out[:, pl.ds(at, stripe)], preferred_element_type=F32)

    sums = {}

    def sum_start(c, s):
        sums[c, s] = [
            remote(
                partial.at[c, s, j],
                inbox.at[c, s, j],
                sum_send.at[c, s, j],
                sum_recv.at[c, s, j],
                {"half": right if j % 2 == 0 else left},
            )
            for j in range(6)
        ]
        for j, (owner, h) in enumerate([(far, 0), (far, 1), (right, 1), (left, 0)]):
            partial[c, s, j] = down(c, s, h, owner).astype(BF16)
            sums[c, s][j].start()

    def sum_middle(c, s):
        for j, (owner, h) in enumerate([(right, 0), (left, 1)]):
            term = down(c, s, h, owner)
            sums[c, s][j].wait_recv()
            partial[c, s, 4 + j] = (term + inbox[c, s, j].astype(F32)).astype(BF16)
            sums[c, s][4 + j].start()

    backs = {}

    def push_back(n, c, start, size):
        cols = pl.ds(start, size)
        there = returned.at[c, pl.ds(y * n_z, n_z), :, cols]

        @pl.loop(1, n_y)
        def _(i):
            peer = lax.rem(y + i, n_y)
            remote(
                done.at[c, pl.ds(peer * n_z, n_z), :, cols],
                there,
                back_send.at[n, c],
                back_recv.at[n, c],
                at_y(i),
            ).start()

        backs[n, c] = pltpu.make_async_copy(
            done.at[c, pl.ds(y * n_z, n_z), :, cols], there, back_local.at[n, c]
        )
        backs[n, c].start()

    def keep_done(c, h, start, size, term):
        done[c, h * half_groups : (h + 1) * half_groups, :, start : start + size] = term.astype(
            BF16
        ).reshape(half_groups, SLOTS, size)

    def sum_end(c, s):
        for h, near, through in ((0, 3, 4), (1, 2, 5)):
            term = down(c, s, h, x)
            sums[c, s][near].wait_recv()
            term = term + inbox[c, s, near].astype(F32)
            sums[c, s][through].wait_recv()
            term = term + inbox[c, s, through].astype(F32)
            keep_done(c, h, s * stripe, stripe, term)
        push_back(s, c, s * stripe, stripe)

    def straight_out(c):
        for h in range(2):
            term = jnp.dot(hidden[c, h], w_out[:, 4 * xw :], preferred_element_type=F32)
            keep_done(c, h, xw, dw, term)
        push_back(stripes, c, xw, dw)

    spans = [(s * stripe, stripe) for s in range(stripes)] + [(xw, dw)]
    downs = {}

    def combine(n):
        start, size = spans[n]
        cols = pl.ds(start, size)
        for c in range(2):
            backs[n, c].wait()
            wait_for(others(returned, c, start, size), back_recv.at[n, c])

        @pl.loop(0, n_z)
        def _(s):
            rows = jnp.concatenate(
                [
                    returned[c, q * n_z + s, :, start : start + size]
                    for c in range(2)
                    for q in range(n_y)
                ],
                axis=0,
            )
            both = jnp.dot(
                weights[s].reshape(2 * tokens, lanes), rows, preferred_element_type=F32
            )
            blend[s, :, start : start + size] = (both[:tokens] + both[tokens:]).astype(BF16)

        @pl.loop(1, n_z)
        def _(i):
            peer = lax.rem(z + i, n_z)
            remote(
                blend.at[peer, :, cols],
                landed.at[z, :, cols],
                down_send.at[n],
                down_recv.at[n],
                at_z(i),
            ).start()

        downs[n] = pltpu.make_async_copy(
            blend.at[z, :, cols], landed.at[z, :, cols], down_local.at[n]
        )
        downs[n].start()

    mixes = {}

    def exchange(n):
        start, size = spans[n]
        cols = pl.ds(start, size)
        downs[n].wait()
        wait_for(landed.at[pl.ds(0, n_z - 1), :, cols], down_recv.at[n])
        total = landed[0, :, start : start + size].astype(F32)
        for s in range(1, n_z):
            total = total + landed[s, :, start : start + size].astype(F32)
        piece[:, start : start + size] = total.astype(BF16)
        for j, where in enumerate((right, left, far)):
            mixes[n, j] = remote(
                piece.at[:, cols],
                gathered.at[j, :, cols],
                mix_send.at[n, j],
                mix_recv.at[n, j],
                {"half": where},
            )
            mixes[n, j].start()

    round_step(0, 0)
    own_select = push_control(0, select, chosen)
    round_step(1, 0)
    for keep in keeps:
        keep.wait()
    for step in range(1, plus):
        round_step(0, step)
        round_step(1, step)
    round_step(0, plus)
    round_step(2, 0)
    round_step(3, 0)
    wait_control(0, own_select, chosen)
    pick(0, width)
    push_y(0, 0, 0, width, mine, 0)
    round_step(1, plus)
    pick(width, width)
    push_y(1, 0, width, width, mine, width)
    push_y(2, 1, 0, width, mine, 0)
    push_y(3, 1, width, width, mine, width)
    round_step(2, 1)
    round_step(3, 1)
    arrive(0)
    round_step(2, 2)
    round_step(3, 2)
    for load in loads[:2]:
        load.wait()
    own(0)
    forward(0)
    arrive(1)
    for step in range(3, plus + 1):
        round_step(2, step)
        round_step(3, step)
    pick(xw, dw)
    push_y(4, 0, xw, dw, direct, 0)
    push_y(5, 1, xw, dw, direct, 0)
    own_gates = push_control(1, gates, weights)
    sides(0)
    arrive(2)
    own(1)
    forward(1)
    opposite(0)
    arrive(3)
    sides(1)
    own(2)
    opposite(1)
    straight(0)
    activate(0)
    loads[2].wait()
    sum_start(0, 0)
    forward(2)
    own(3)
    sum_start(0, 1)
    sum_middle(0, 0)
    forward(3)
    straight_out(0)
    sides(2)
    opposite(2)
    sum_middle(0, 1)
    sum_end(0, 0)
    straight(1)
    sides(3)
    opposite(3)
    activate(1)
    sum_start(1, 0)
    sum_end(0, 1)
    straight_out(1)
    sum_middle(1, 0)
    sum_start(1, 1)
    sum_start(0, 2)
    sum_end(1, 0)
    sum_middle(1, 1)
    wait_control(1, own_gates, weights)
    combine(stripes)
    sum_start(1, 2)
    sum_middle(0, 2)
    combine(0)
    sum_end(1, 1)
    sum_end(0, 2)
    sum_middle(1, 2)
    exchange(stripes)
    combine(1)
    exchange(0)
    sum_end(1, 2)
    exchange(1)
    combine(2)
    exchange(2)
    for n in range(stripes + 1):
        for j in range(3):
            mixes[n, j].wait_recv()
    result[:, pl.ds(pl.multiple_of(x * xw, 128), xw)] = piece[:, :xw]
    shared = piece[:, xw:].astype(F32)
    for j, owner in enumerate((left, right, far)):
        result[:, pl.ds(pl.multiple_of(owner * xw, 128), xw)] = gathered[j, :, :xw]
        shared = shared + gathered[j, :, xw:].astype(F32)
    result[:, 4 * xw :] = shared.astype(BF16)
    for p in range(4):
        for way, steps in ((0, plus), (1, minus)):
            for step in range(steps):
                trips[p, way, step].wait_send()
    wait_for(chosen.at[pl.ds(0, n_z - 1)], ctl_send.at[0])
    wait_for(weights.at[pl.ds(0, n_z - 1)], ctl_send.at[1])
    for k in range(4):
        wait_for(others(mine, k // 2, k % 2 * width, width), y_send.at[k])
        for j in range(6):
            ring[k][j].wait_send()
    for c in range(2):
        wait_for(others(direct, c, 0, dw), y_send.at[4 + c])
        for n, (start, size) in enumerate(spans):
            wait_for(others(returned, c, start, size), back_send.at[n, c])
        for s in range(stripes):
            for j in range(6):
                sums[c, s][j].wait_send()
    for n, (start, size) in enumerate(spans):
        wait_for(landed.at[pl.ds(0, n_z - 1), :, pl.ds(start, size)], down_send.at[n])
        for j in range(3):
            mixes[n, j].wait_send()


def experts(tok, routes, router, w_gate, w_up, w_down, n_z, stripes):
    model, ff = w_gate.shape
    tokens, n_ep = tok.shape[0], router.shape[0]
    xw = model * 3 // 16
    dw = model - 4 * xw
    columns = xw + dw
    n_y = n_ep // n_z
    lanes = 2 * n_y * SLOTS
    half_rows = n_ep // 2 * SLOTS
    dma = pltpu.SemaphoreType.DMA
    vmem = pl.BlockSpec(memory_space=pltpu.VMEM)
    hbm = pl.BlockSpec(memory_space=pl.ANY)

    def space(*shape, dtype=BF16):
        return pltpu.VMEM(shape, dtype)

    return pl.pallas_call(
        moe_kernel,
        out_shape=jax.ShapeDtypeStruct((tokens, model), BF16),
        in_specs=[vmem, vmem, hbm, hbm, hbm, hbm],
        out_specs=vmem,
        scratch_shapes=[
            space(n_ep, model),
            space(1, tokens, n_ep * CAP),
            space(2, tokens, n_ep * CAP),
            space(model, 2 * ff),
            space(ff, model),
            space(n_z, tokens, columns),
            space(n_z, 1, tokens, lanes),
            space(n_z, 2, tokens, lanes),
            space(2, n_y, n_z, SLOTS, columns),
            space(2, n_ep, SLOTS, xw),
            space(2, n_ep, SLOTS, dw),
            space(2, n_ep, SLOTS, xw),
            space(2, n_ep, SLOTS, xw),
            space(2, n_ep, SLOTS, xw),
            space(2, 2, half_rows, 2 * ff, dtype=F32),
            space(2, 2, half_rows, ff),
            space(2, stripes, 6, half_rows, xw // stripes),
            space(2, stripes, 6, half_rows, xw // stripes),
            space(2, n_ep, SLOTS, columns),
            space(2, n_ep, SLOTS, columns),
            space(n_z, tokens, columns),
            space(n_z, tokens, columns),
            space(tokens, columns),
            space(3, tokens, columns),
            dma((4,)),
            dma((2,)),
            dma((4, 2, n_z // 2)),
            dma((4, 2, n_z // 2)),
            dma((2,)),
            dma((2,)),
            dma((2,)),
            dma((6,)),
            dma((6,)),
            dma((6,)),
            dma((4, 6)),
            dma((4, 6)),
            dma((2, stripes, 6)),
            dma((2, stripes, 6)),
            dma((stripes + 1, 2)),
            dma((stripes + 1, 2)),
            dma((stripes + 1, 2)),
            dma((stripes + 1,)),
            dma((stripes + 1,)),
            dma((stripes + 1,)),
            dma((stripes + 1, 3)),
            dma((stripes + 1, 3)),
        ],
        compiler_params=pltpu.CompilerParams(
            collective_id=0, has_side_effects=True, vmem_limit_bytes=58 * 2**20
        ),
        cost_estimate=pl.CostEstimate(
            flops=12 * n_ep * SLOTS * model * ff,
            bytes_accessed=6 * model * ff + 500 * 2**20,
            transcendentals=2 * n_ep * SLOTS * ff,
        ),
        name="experts",
    )(tok, routes, router, w_gate, w_up, w_down)


def decode_kernel(
    tok,
    moe,
    gain,
    w_kv,
    allowed,
    queries,
    new_keys,
    new_values,
    w_out,
    result,
    w_kv_here,
    w_out_here,
    own_kv,
    other_kv,
    heads,
    partial,
    inbox,
    load_sem,
    swap_send,
    swap_recv,
    send_sem,
    recv_sem,
):
    x = lax.axis_index("half")
    right = lax.rem(x + 1, 4)
    left = lax.rem(x + 3, 4)
    far = lax.rem(x + 2, 4)
    partner = {"pool": 1 - lax.axis_index("pool")}
    load_kv = pltpu.make_async_copy(w_kv, w_kv_here, load_sem.at[0])
    load_out = pltpu.make_async_copy(w_out, w_out_here, load_sem.at[1])
    load_kv.start()
    load_out.start()
    barrier = pltpu.get_barrier_semaphore()
    pl.semaphore_signal(barrier, inc=1, device_id=partner, device_id_type=MESH)
    for peer in (left, right, far):
        pl.semaphore_signal(barrier, inc=1, device_id={"half": peer}, device_id_type=MESH)

    mixed = tok[...].astype(F32) + moe[...].astype(F32)
    meansq = jnp.mean(mixed * mixed, axis=1, keepdims=True)
    normed = (mixed * lax.rsqrt(meansq + 1e-06) * gain[...]).astype(BF16)
    load_kv.wait()
    own_kv[...] = jnp.dot(normed, w_kv_here[...], preferred_element_type=F32).astype(BF16)
    pl.semaphore_wait(barrier, 4)
    swap = pltpu.make_async_remote_copy(
        src_ref=own_kv,
        dst_ref=other_kv,
        send_sem=swap_send,
        recv_sem=swap_recv,
        device_id=partner,
        device_id_type=MESH,
    )
    swap.start()
    rows = queries.shape[0] // 4
    kv_heads = new_keys.shape[1] // HEAD
    shared = queries.shape[1] // new_keys.shape[1]
    scale = 1.0 / math.sqrt(HEAD)
    swap.wait_recv()
    load_out.wait()

    def block(owner):
        at = pl.ds(pl.multiple_of(owner * rows, rows), rows)
        seen = allowed[at, :] > 0.0
        for h in range(kv_heads):
            keys = other_kv[:, 2 * h * HEAD : (2 * h + 1) * HEAD]
            values = other_kv[:, (2 * h + 1) * HEAD : (2 * h + 2) * HEAD]
            fresh_key = new_keys[at, h * HEAD : (h + 1) * HEAD].astype(F32)
            fresh_value = new_values[at, h * HEAD : (h + 1) * HEAD].astype(F32)
            for g in range(shared):
                cols = slice((h * shared + g) * HEAD, (h * shared + g + 1) * HEAD)
                query = queries[at, cols]
                scores = lax.dot_general(
                    query, keys, (((1,), (1,)), ((), ())), preferred_element_type=F32
                )
                scores = jnp.where(seen, scores * scale, -1e30)
                own = jnp.sum(query.astype(F32) * fresh_key, axis=1, keepdims=True) * scale
                top = jnp.maximum(jnp.max(scores, axis=1, keepdims=True), own)
                spread = jnp.where(seen, jnp.exp(scores - top), 0.0)
                self_weight = jnp.exp(own - top)
                total = jnp.sum(spread, axis=1, keepdims=True) + self_weight
                probs = (spread / total).astype(BF16)
                self_prob = (self_weight / total).astype(BF16).astype(F32)
                value = jnp.dot(probs, values, preferred_element_type=F32)
                heads[:, cols] = (value + self_prob * fresh_value).astype(BF16)
        return jnp.dot(heads[...], w_out_here[...], preferred_element_type=F32)

    copies = []
    for j, owner in enumerate((far, right, left)):
        partial[j] = block(owner).astype(BF16)
        copy = pltpu.make_async_remote_copy(
            src_ref=partial.at[j],
            dst_ref=inbox.at[j],
            send_sem=send_sem.at[j],
            recv_sem=recv_sem.at[j],
            device_id={"half": owner},
            device_id_type=MESH,
        )
        copy.start()
        copies.append(copy)
    total = block(x).astype(BF16).astype(F32)
    for j in (1, 2, 0):
        copies[j].wait_recv()
        total = total + inbox[j].astype(F32)
    result[...] = total.astype(BF16)
    swap.wait_send()
    for copy in copies:
        copy.wait_send()


def decode(tok, moe, gain, w_kv, allowed, queries, new_keys, new_values, w_out):
    rows, inner = queries.shape[0] // 4, queries.shape[1]
    wide = w_out.shape[1]
    dma = pltpu.SemaphoreType.DMA
    vmem = pl.BlockSpec(memory_space=pltpu.VMEM)
    hbm = pl.BlockSpec(memory_space=pl.ANY)
    return pl.pallas_call(
        decode_kernel,
        out_shape=jax.ShapeDtypeStruct((rows, wide), BF16),
        in_specs=[vmem, vmem, vmem, hbm, vmem, vmem, vmem, vmem, hbm],
        out_specs=vmem,
        scratch_shapes=[
            pltpu.VMEM(w_kv.shape, BF16),
            pltpu.VMEM(w_out.shape, BF16),
            pltpu.VMEM((tok.shape[0], w_kv.shape[1]), BF16),
            pltpu.VMEM((tok.shape[0], w_kv.shape[1]), BF16),
            pltpu.VMEM((rows, inner), BF16),
            pltpu.VMEM((3, rows, wide), BF16),
            pltpu.VMEM((3, rows, wide), BF16),
            dma((2,)),
            dma,
            dma,
            dma((3,)),
            dma((3,)),
        ],
        compiler_params=pltpu.CompilerParams(
            collective_id=1, has_side_effects=True, vmem_limit_bytes=58 * 2**20
        ),
        cost_estimate=pl.CostEstimate(
            flops=2 * tok.shape[0] * w_kv.size + 8 * rows * w_out.size,
            bytes_accessed=2 * (w_kv.size + w_out.size),
            transcendentals=8 * rows * tok.shape[0] * 8,
        ),
        name="decode",
    )(tok, moe, gain, w_kv, allowed, queries, new_keys, new_values, w_out)


def on_device(
    tokens,
    routes,
    router,
    w_gate,
    w_up,
    w_down,
    norm_gain,
    w_kv,
    lengths,
    queries,
    new_keys,
    new_values,
    w_out,
):
    inputs = tokens[0]
    moe = experts(inputs, routes[0].T, router.T, w_gate[0], w_up[0], w_down[0], RING, 3)
    rows = w_kv.shape[0] // 2
    pool = lax.axis_index("pool")
    mine = lax.dynamic_slice_in_dim(w_kv, pool * rows, rows, 0)
    w_all = lax.all_gather(mine, ("ep", "pool"), axis=0, tiled=True)
    first = lax.dynamic_slice(lengths, (1 - pool, 0, 0), (1, 1, 1))[0]
    second = jnp.arange(inputs.shape[0], dtype=jnp.int32)[None, :] >= first
    prompt = jnp.arange(queries.shape[1], dtype=jnp.int32)[:, None] // SAMPLES
    allowed = (second == (prompt == 1)).astype(F32)
    return decode(
        inputs, moe, norm_gain[None], w_all, allowed, queries[0], new_keys[0], new_values[0], w_out
    )[None]


def solution(mesh):
    in_specs = (
        P("pool", "ep", None),
        P("pool", "ep", None),
        P(),
        P("ep", None, "half"),
        P("ep", None, "half"),
        P("ep", "half", None),
        P(),
        P("ep", "half"),
        P(None, "ep", None),
        P("pool", "ep", "half"),
        P("pool", "ep", "half"),
        P("pool", "ep", "half"),
        P("half", None),
    )
    out_specs = P("pool", ("ep", "half"), None)
    return jax.shard_map(
        on_device, mesh=mesh, in_specs=in_specs, out_specs=out_specs, check_vma=False
    )
```

```python
import math

import jax
import jax.numpy as jnp
from jax import lax
from jax.experimental import pallas as pl
from jax.experimental.pallas import tpu as pltpu
from jax.sharding import PartitionSpec as P

HEAD = 128
SAMPLES = 128
CAP = 32
SLOTS = 16
RING = 8
MESH = pl.DeviceIdType.MESH
BF16 = jnp.bfloat16
F32 = jnp.float32


def moe_kernel(
    tok,
    routes,
    router,
    w_gate,
    w_up,
    w_down,
    result,
    router_here,
    select,
    gates,
    w_in,
    w_out,
    held,
    chosen,
    weights,
    picked,
    mine,
    direct,
    from_left,
    from_right,
    from_far,
    acc,
    hidden,
    partial,
    inbox,
    done,
    returned,
    blend,
    landed,
    piece,
    gathered,
    w_sem,
    tok_sem,
    zring_send,
    zring_recv,
    ctl_local,
    ctl_send,
    ctl_recv,
    y_local,
    y_send,
    y_recv,
    ring_send,
    ring_recv,
    sum_send,
    sum_recv,
    back_local,
    back_send,
    back_recv,
    down_local,
    down_send,
    down_recv,
    mix_send,
    mix_recv,
):
    tokens = tok.shape[0]
    columns = held.shape[2]
    xw = from_left.shape[3]
    dw = columns - xw
    width = xw // 2
    ff = w_gate.shape[1]
    n_ep = mine.shape[1]
    n_z = held.shape[0]
    n_y = n_ep // n_z
    half_groups = n_ep // 2
    half_rows = half_groups * SLOTS
    stripes = partial.shape[1]
    stripe = xw // stripes
    lanes = 2 * n_y * SLOTS
    ep = lax.axis_index("ep")
    y = ep // n_z
    z = lax.rem(ep, n_z)
    x = lax.axis_index("half")
    right = lax.rem(x + 1, 4)
    left = lax.rem(x + 3, 4)
    far = lax.rem(x + 2, 4)

    def at_z(i):
        return {"ep": y * n_z + lax.rem(z + i, n_z)}

    def at_y(i):
        return {"ep": lax.rem(y + i, n_y) * n_z + z}

    loads = [
        pltpu.make_async_copy(w_gate, w_in.at[:, pl.ds(0, ff)], w_sem.at[0]),
        pltpu.make_async_copy(w_up, w_in.at[:, pl.ds(ff, ff)], w_sem.at[1]),
        pltpu.make_async_copy(w_down, w_out, w_sem.at[2]),
    ]
    for load in loads:
        load.start()
    load_router = pltpu.make_async_copy(router, router_here, w_sem.at[3])
    load_router.start()
    own_cols = pl.ds(pl.multiple_of(x * xw, 128), xw)
    keeps = [
        pltpu.make_async_copy(tok.at[:, own_cols], held.at[z, :, pl.ds(0, xw)], tok_sem.at[0]),
        pltpu.make_async_copy(
            tok.at[:, pl.ds(4 * xw, dw)], held.at[z, :, pl.ds(xw, dw)], tok_sem.at[1]
        ),
    ]
    for keep in keeps:
        keep.start()

    barrier = pltpu.get_barrier_semaphore()

    def greet(where):
        pl.semaphore_signal(barrier, inc=1, device_id=where, device_id_type=MESH)

    @pl.loop(1, n_z)
    def _(i):
        greet(at_z(i))

    @pl.loop(1, n_y)
    def _(i):
        greet(at_y(i))

    for peer in (left, right, far):
        greet({"half": peer})

    load_router.wait()
    logits = lax.dot_general(
        tok[...], router_here[...], (((1,), (1,)), ((), ())), preferred_element_type=F32
    )
    expert = lax.broadcasted_iota(jnp.int32, (n_ep, tokens), 0)
    naming = jnp.zeros((n_ep, tokens), F32)
    for k in range(routes.shape[0]):
        naming = naming + jnp.where(routes[k : k + 1, :] == expert, 1.0, 0.0)
    row = lax.broadcasted_iota(jnp.int32, (tokens, tokens), 0)
    column = lax.broadcasted_iota(jnp.int32, (tokens, tokens), 1)

    def by_token(pairs):
        return lax.dot_general(
            jnp.where(pairs, 1.0, 0.0).astype(BF16),
            naming.astype(BF16),
            (((1,), (1,)), ((), ())),
            preferred_element_type=F32,
        )

    named = by_token(column == row)
    rank = by_token(column < row)
    top = jnp.max(jnp.where(named > 0.0, logits, -jnp.inf), axis=1, keepdims=True)
    spread = jnp.where(named > 0.0, jnp.exp(jnp.minimum(logits - top, 0.0)), 0.0)
    gate_of = spread / jnp.sum(spread, axis=1, keepdims=True)
    coarse = gate_of.astype(BF16)
    fine = (gate_of - coarse.astype(F32)).astype(BF16)

    def bits(value, size):
        return lax.shift_right_logical(value, jnp.int32(size.bit_length() - 1))

    def slot_facts(count):
        lane = lax.broadcasted_iota(jnp.int32, (count, n_ep * CAP), 1)
        inner = lane & (lanes - 1)
        whose = (bits(inner, SLOTS) & (n_y - 1)) * n_z + bits(lane, lanes)
        return whose, bits(inner, n_y * SLOTS) * SLOTS + (inner & (SLOTS - 1))

    whose, _ = slot_facts(n_ep)
    spreader = jnp.where(
        whose == lax.broadcasted_iota(jnp.int32, whose.shape, 0), 1.0, 0.0
    ).astype(BF16)

    def to_slots(table):
        return jnp.dot(table.astype(BF16), spreader, preferred_element_type=F32)

    _, place = slot_facts(tokens)
    held_here = (to_slots(named) > 0.0) & (to_slots(rank) == place.astype(F32))
    select[0] = jnp.where(held_here, 1.0, 0.0).astype(BF16)
    gates[0] = jnp.where(held_here, to_slots(coarse), 0.0).astype(BF16)
    gates[1] = jnp.where(held_here, to_slots(fine), 0.0).astype(BF16)
    pl.semaphore_wait(barrier, n_z + n_y + 1)

    def remote(src, dst, sems, recvs, where):
        return pltpu.make_async_remote_copy(
            src_ref=src,
            dst_ref=dst,
            send_sem=sems,
            recv_sem=recvs,
            device_id=where,
            device_id_type=MESH,
        )

    def wait_for(block, sem):
        pltpu.make_async_copy(block, block, sem).wait()

    parts = [(0, width), (width, width), (xw, dw // 2), (xw + dw // 2, dw // 2)]
    plus = n_z // 2
    minus = n_z - 1 - plus

    def round_copy(p, way, step):
        start, size = parts[p]
        cols = pl.ds(start, size)
        back = n_z - step if way == 0 else step
        block = lax.rem(z + back, n_z)
        if step == 0:
            base = x * xw + start if start < xw else 3 * xw + start
            src = tok.at[:, pl.ds(pl.multiple_of(base, 128), size)]
        else:
            src = held.at[block, :, cols]
        return remote(
            src,
            held.at[block, :, cols],
            zring_send.at[p, way, step],
            zring_recv.at[p, way, step],
            at_z(1 if way == 0 else n_z - 1),
        )

    trips = {}

    def round_step(p, step):
        for way, steps in ((0, plus), (1, minus)):
            if 0 < step <= steps:
                trips[p, way, step - 1].wait_recv()
            if step < steps:
                trips[p, way, step] = round_copy(p, way, step)
                trips[p, way, step].start()

    def push_control(n, src, dst):
        @pl.loop(1, n_z)
        def _(i):
            there = pl.multiple_of(lax.rem(z + i, n_z) * lanes, lanes)
            remote(
                src.at[:, :, pl.ds(there, lanes)], dst.at[z], ctl_send.at[n], ctl_recv.at[n], at_z(i)
            ).start()

        here = pl.multiple_of(z * lanes, lanes)
        own = pltpu.make_async_copy(src.at[:, :, pl.ds(here, lanes)], dst.at[z], ctl_local.at[n])
        own.start()
        return own

    def wait_control(n, own, dst):
        own.wait()
        wait_for(dst.at[pl.ds(0, n_z - 1)], ctl_recv.at[n])

    def pick(start, size):
        @pl.loop(0, n_z)
        def _(s):
            rows = lax.dot_general(
                chosen[s, 0],
                held[s, :, start : start + size],
                (((0,), (0,)), ((), ())),
                preferred_element_type=F32,
            ).astype(BF16)
            rows = rows.reshape(2 * n_y, SLOTS, size)
            for b in range(2 * n_y):
                picked[b // n_y, b % n_y, s, :, start : start + size] = rows[b]

    y_own = {}

    def push_y(n, c, start, size, dst, dst_start):
        cols = pl.ds(start, size)
        there = dst.at[c, pl.ds(y * n_z, n_z), :, pl.ds(dst_start, size)]

        @pl.loop(1, n_y)
        def _(i):
            peer = lax.rem(y + i, n_y)
            remote(
                picked.at[c, peer, :, :, cols], there, y_send.at[n], y_recv.at[n], at_y(i)
            ).start()

        y_own[n] = pltpu.make_async_copy(picked.at[c, y, :, :, cols], there, y_local.at[n])
        y_own[n].start()

    def others(ref, c, start, size):
        return ref.at[c, pl.ds(0, n_ep - n_z), :, pl.ds(start, size)]

    def stage(k):
        return k // 2, pl.ds(k % 2 * width, width)

    def half_of(ref, k, h):
        c, cols = stage(k)
        return ref.at[c, pl.ds(h * half_groups, half_groups), :, cols]

    ring = {}

    def arrive(k):
        y_own[k].wait()
        wait_for(others(mine, k // 2, k % 2 * width, width), y_recv.at[k])
        plan = [
            (half_of(mine, k, 0), half_of(from_left, k, 0), right),
            (half_of(mine, k, 1), half_of(from_right, k, 1), left),
            (half_of(mine, k, 1), half_of(from_left, k, 1), right),
            (half_of(mine, k, 0), half_of(from_right, k, 0), left),
            (half_of(from_left, k, 0), half_of(from_far, k, 0), right),
            (half_of(from_right, k, 1), half_of(from_far, k, 1), left),
        ]
        ring[k] = [
            remote(src, dst, ring_send.at[k, j], ring_recv.at[k, j], {"half": where})
            for j, (src, dst, where) in enumerate(plan)
        ]
        for j in range(4):
            ring[k][j].start()

    def forward(k):
        ring[k][0].wait_recv()
        ring[k][4].start()
        ring[k][1].wait_recv()
        ring[k][5].start()

    def accumulate(ref, c, h, start, size, at, first=False):
        rows = ref[c, h * half_groups : (h + 1) * half_groups, :, start : start + size]
        term = jnp.dot(
            rows.reshape(half_rows, size), w_in[pl.ds(at, size), :], preferred_element_type=F32
        )
        if first:
            acc[c, h] = term
        else:
            acc[c, h] += term

    def add(ref, k, h, owner, first=False):
        at = pl.multiple_of(owner * xw + k % 2 * width, 128)
        accumulate(ref, k // 2, h, k % 2 * width, width, at, first)

    def own(k):
        for h in range(2):
            add(mine, k, h, x, first=k % 2 == 0)

    def sides(k):
        add(from_left, k, 0, left)
        add(from_right, k, 1, right)
        ring[k][2].wait_recv()
        add(from_left, k, 1, left)
        ring[k][3].wait_recv()
        add(from_right, k, 0, right)

    def opposite(k):
        ring[k][4].wait_recv()
        add(from_far, k, 0, far)
        ring[k][5].wait_recv()
        add(from_far, k, 1, far)

    def straight(c):
        y_own[4 + c].wait()
        wait_for(others(direct, c, 0, dw), y_recv.at[4 + c])
        for h in range(2):
            accumulate(direct, c, h, 0, dw, 4 * xw)

    def activate(c):
        for h in range(2):
            gate = acc[c, h, :, :ff]
            up = acc[c, h, :, ff:]
            hidden[c, h] = (gate / (1.0 + jnp.exp(-gate)) * up).astype(BF16)

    def down(c, s, h, owner):
        at = pl.multiple_of(owner * xw + s * stripe, 128)
        return jnp.dot(hidden[c, h], w_out[:, pl.ds(at, stripe)], preferred_element_type=F32)

    sums = {}

    def sum_start(c, s):
        sums[c, s] = [
            remote(
                partial.at[c, s, j],
                inbox.at[c, s, j],
                sum_send.at[c, s, j],
                sum_recv.at[c, s, j],
                {"half": right if j % 2 == 0 else left},
            )
            for j in range(6)
        ]
        for j, (owner, h) in enumerate([(far, 0), (far, 1), (right, 1), (left, 0)]):
            partial[c, s, j] = down(c, s, h, owner).astype(BF16)
            sums[c, s][j].start()

    def sum_middle(c, s):
        for j, (owner, h) in enumerate([(right, 0), (left, 1)]):
            term = down(c, s, h, owner)
            sums[c, s][j].wait_recv()
            partial[c, s, 4 + j] = (term + inbox[c, s, j].astype(F32)).astype(BF16)
            sums[c, s][4 + j].start()

    backs = {}

    def push_back(n, c, start, size):
        cols = pl.ds(start, size)
        there = returned.at[c, pl.ds(y * n_z, n_z), :, cols]

        @pl.loop(1, n_y)
        def _(i):
            peer = lax.rem(y + i, n_y)
            remote(
                done.at[c, pl.ds(peer * n_z, n_z), :, cols],
                there,
                back_send.at[n, c],
                back_recv.at[n, c],
                at_y(i),
            ).start()

        backs[n, c] = pltpu.make_async_copy(
            done.at[c, pl.ds(y * n_z, n_z), :, cols], there, back_local.at[n, c]
        )
        backs[n, c].start()

    def keep_done(c, h, start, size, term):
        done[c, h * half_groups : (h + 1) * half_groups, :, start : start + size] = term.astype(
            BF16
        ).reshape(half_groups, SLOTS, size)

    def sum_end(c, s):
        for h, near, through in ((0, 3, 4), (1, 2, 5)):
            term = down(c, s, h, x)
            sums[c, s][near].wait_recv()
            term = term + inbox[c, s, near].astype(F32)
            sums[c, s][through].wait_recv()
            term = term + inbox[c, s, through].astype(F32)
            keep_done(c, h, s * stripe, stripe, term)
        push_back(s, c, s * stripe, stripe)

    def straight_out(c):
        for h in range(2):
            term = jnp.dot(hidden[c, h], w_out[:, 4 * xw :], preferred_element_type=F32)
            keep_done(c, h, xw, dw, term)
        push_back(stripes, c, xw, dw)

    spans = [(s * stripe, stripe) for s in range(stripes)] + [(xw, dw)]
    downs = {}

    def combine(n):
        start, size = spans[n]
        cols = pl.ds(start, size)
        for c in range(2):
            backs[n, c].wait()
            wait_for(others(returned, c, start, size), back_recv.at[n, c])

        @pl.loop(0, n_z)
        def _(s):
            rows = jnp.concatenate(
                [
                    returned[c, q * n_z + s, :, start : start + size]
                    for c in range(2)
                    for q in range(n_y)
                ],
                axis=0,
            )
            both = jnp.dot(
                weights[s].reshape(2 * tokens, lanes), rows, preferred_element_type=F32
            )
            blend[s, :, start : start + size] = (both[:tokens] + both[tokens:]).astype(BF16)

        @pl.loop(1, n_z)
        def _(i):
            peer = lax.rem(z + i, n_z)
            remote(
                blend.at[peer, :, cols],
                landed.at[z, :, cols],
                down_send.at[n],
                down_recv.at[n],
                at_z(i),
            ).start()

        downs[n] = pltpu.make_async_copy(
            blend.at[z, :, cols], landed.at[z, :, cols], down_local.at[n]
        )
        downs[n].start()

    mixes = {}

    def exchange(n):
        start, size = spans[n]
        cols = pl.ds(start, size)
        downs[n].wait()
        wait_for(landed.at[pl.ds(0, n_z - 1), :, cols], down_recv.at[n])
        total = landed[0, :, start : start + size].astype(F32)
        for s in range(1, n_z):
            total = total + landed[s, :, start : start + size].astype(F32)
        piece[:, start : start + size] = total.astype(BF16)
        for j, where in enumerate((right, left, far)):
            mixes[n, j] = remote(
                piece.at[:, cols],
                gathered.at[j, :, cols],
                mix_send.at[n, j],
                mix_recv.at[n, j],
                {"half": where},
            )
            mixes[n, j].start()

    round_step(0, 0)
    own_select = push_control(0, select, chosen)
    round_step(1, 0)
    for keep in keeps:
        keep.wait()
    for step in range(1, plus):
        round_step(0, step)
        round_step(1, step)
    round_step(0, plus)
    round_step(2, 0)
    round_step(3, 0)
    wait_control(0, own_select, chosen)
    pick(0, width)
    push_y(0, 0, 0, width, mine, 0)
    round_step(1, plus)
    round_step(2, 1)
    round_step(3, 1)
    pick(width, width)
    push_y(1, 0, width, width, mine, width)
    push_y(2, 1, 0, width, mine, 0)
    push_y(3, 1, width, width, mine, width)
    round_step(2, 2)
    round_step(3, 2)
    arrive(0)
    for step in range(3, plus):
        round_step(2, step)
        round_step(3, step)
    for load in loads[:2]:
        load.wait()
    own(0)
    round_step(2, plus)
    round_step(3, plus)
    forward(0)
    arrive(1)
    pick(xw, dw)
    push_y(4, 0, xw, dw, direct, 0)
    push_y(5, 1, xw, dw, direct, 0)
    own_gates = push_control(1, gates, weights)
    sides(0)
    arrive(2)
    own(1)
    forward(1)
    opposite(0)
    arrive(3)
    sides(1)
    own(2)
    opposite(1)
    straight(0)
    activate(0)
    loads[2].wait()
    sum_start(0, 0)
    forward(2)
    own(3)
    sum_start(0, 1)
    sum_middle(0, 0)
    forward(3)
    straight_out(0)
    sides(2)
    opposite(2)
    sum_middle(0, 1)
    sum_end(0, 0)
    straight(1)
    sides(3)
    opposite(3)
    activate(1)
    sum_start(1, 0)
    sum_end(0, 1)
    straight_out(1)
    sum_middle(1, 0)
    sum_start(1, 1)
    sum_start(0, 2)
    sum_end(1, 0)
    sum_middle(1, 1)
    wait_control(1, own_gates, weights)
    combine(stripes)
    sum_start(1, 2)
    sum_middle(0, 2)
    combine(0)
    sum_end(1, 1)
    sum_end(0, 2)
    sum_middle(1, 2)
    exchange(stripes)
    combine(1)
    exchange(0)
    sum_end(1, 2)
    exchange(1)
    combine(2)
    exchange(2)
    for n in range(stripes + 1):
        for j in range(3):
            mixes[n, j].wait_recv()
    result[:, pl.ds(pl.multiple_of(x * xw, 128), xw)] = piece[:, :xw]
    shared = piece[:, xw:].astype(F32)
    for j, owner in enumerate((left, right, far)):
        result[:, pl.ds(pl.multiple_of(owner * xw, 128), xw)] = gathered[j, :, :xw]
        shared = shared + gathered[j, :, xw:].astype(F32)
    result[:, 4 * xw :] = shared.astype(BF16)
    for p in range(4):
        for way, steps in ((0, plus), (1, minus)):
            for step in range(steps):
                trips[p, way, step].wait_send()
    wait_for(chosen.at[pl.ds(0, n_z - 1)], ctl_send.at[0])
    wait_for(weights.at[pl.ds(0, n_z - 1)], ctl_send.at[1])
    for k in range(4):
        wait_for(others(mine, k // 2, k % 2 * width, width), y_send.at[k])
        for j in range(6):
            ring[k][j].wait_send()
    for c in range(2):
        wait_for(others(direct, c, 0, dw), y_send.at[4 + c])
        for n, (start, size) in enumerate(spans):
            wait_for(others(returned, c, start, size), back_send.at[n, c])
        for s in range(stripes):
            for j in range(6):
                sums[c, s][j].wait_send()
    for n, (start, size) in enumerate(spans):
        wait_for(landed.at[pl.ds(0, n_z - 1), :, pl.ds(start, size)], down_send.at[n])
        for j in range(3):
            mixes[n, j].wait_send()


def experts(tok, routes, router, w_gate, w_up, w_down, n_z, stripes):
    model, ff = w_gate.shape
    tokens, n_ep = tok.shape[0], router.shape[0]
    xw = model * 3 // 16
    dw = model - 4 * xw
    columns = xw + dw
    n_y = n_ep // n_z
    lanes = 2 * n_y * SLOTS
    half_rows = n_ep // 2 * SLOTS
    dma = pltpu.SemaphoreType.DMA
    vmem = pl.BlockSpec(memory_space=pltpu.VMEM)
    hbm = pl.BlockSpec(memory_space=pl.ANY)

    def space(*shape, dtype=BF16):
        return pltpu.VMEM(shape, dtype)

    return pl.pallas_call(
        moe_kernel,
        out_shape=jax.ShapeDtypeStruct((tokens, model), BF16),
        in_specs=[vmem, vmem, hbm, hbm, hbm, hbm],
        out_specs=vmem,
        scratch_shapes=[
            space(n_ep, model),
            space(1, tokens, n_ep * CAP),
            space(2, tokens, n_ep * CAP),
            space(model, 2 * ff),
            space(ff, model),
            space(n_z, tokens, columns),
            space(n_z, 1, tokens, lanes),
            space(n_z, 2, tokens, lanes),
            space(2, n_y, n_z, SLOTS, columns),
            space(2, n_ep, SLOTS, xw),
            space(2, n_ep, SLOTS, dw),
            space(2, n_ep, SLOTS, xw),
            space(2, n_ep, SLOTS, xw),
            space(2, n_ep, SLOTS, xw),
            space(2, 2, half_rows, 2 * ff, dtype=F32),
            space(2, 2, half_rows, ff),
            space(2, stripes, 6, half_rows, xw // stripes),
            space(2, stripes, 6, half_rows, xw // stripes),
            space(2, n_ep, SLOTS, columns),
            space(2, n_ep, SLOTS, columns),
            space(n_z, tokens, columns),
            space(n_z, tokens, columns),
            space(tokens, columns),
            space(3, tokens, columns),
            dma((4,)),
            dma((2,)),
            dma((4, 2, n_z // 2)),
            dma((4, 2, n_z // 2)),
            dma((2,)),
            dma((2,)),
            dma((2,)),
            dma((6,)),
            dma((6,)),
            dma((6,)),
            dma((4, 6)),
            dma((4, 6)),
            dma((2, stripes, 6)),
            dma((2, stripes, 6)),
            dma((stripes + 1, 2)),
            dma((stripes + 1, 2)),
            dma((stripes + 1, 2)),
            dma((stripes + 1,)),
            dma((stripes + 1,)),
            dma((stripes + 1,)),
            dma((stripes + 1, 3)),
            dma((stripes + 1, 3)),
        ],
        compiler_params=pltpu.CompilerParams(
            collective_id=0, has_side_effects=True, vmem_limit_bytes=58 * 2**20
        ),
        cost_estimate=pl.CostEstimate(
            flops=12 * n_ep * SLOTS * model * ff,
            bytes_accessed=6 * model * ff + 500 * 2**20,
            transcendentals=2 * n_ep * SLOTS * ff,
        ),
        name="experts",
    )(tok, routes, router, w_gate, w_up, w_down)


def decode_kernel(
    tok,
    moe,
    gain,
    w_kv,
    allowed,
    queries,
    new_keys,
    new_values,
    w_out,
    result,
    w_kv_here,
    w_out_here,
    own_kv,
    other_kv,
    heads,
    partial,
    inbox,
    load_sem,
    swap_send,
    swap_recv,
    send_sem,
    recv_sem,
):
    x = lax.axis_index("half")
    right = lax.rem(x + 1, 4)
    left = lax.rem(x + 3, 4)
    far = lax.rem(x + 2, 4)
    partner = {"pool": 1 - lax.axis_index("pool")}
    load_kv = pltpu.make_async_copy(w_kv, w_kv_here, load_sem.at[0])
    load_out = pltpu.make_async_copy(w_out, w_out_here, load_sem.at[1])
    load_kv.start()
    load_out.start()
    barrier = pltpu.get_barrier_semaphore()
    pl.semaphore_signal(barrier, inc=1, device_id=partner, device_id_type=MESH)
    for peer in (left, right, far):
        pl.semaphore_signal(barrier, inc=1, device_id={"half": peer}, device_id_type=MESH)

    mixed = tok[...].astype(F32) + moe[...].astype(F32)
    meansq = jnp.mean(mixed * mixed, axis=1, keepdims=True)
    normed = (mixed * lax.rsqrt(meansq + 1e-06) * gain[...]).astype(BF16)
    load_kv.wait()
    own_kv[...] = jnp.dot(normed, w_kv_here[...], preferred_element_type=F32).astype(BF16)
    pl.semaphore_wait(barrier, 4)
    swap = pltpu.make_async_remote_copy(
        src_ref=own_kv,
        dst_ref=other_kv,
        send_sem=swap_send,
        recv_sem=swap_recv,
        device_id=partner,
        device_id_type=MESH,
    )
    swap.start()
    rows = queries.shape[0] // 4
    kv_heads = new_keys.shape[1] // HEAD
    shared = queries.shape[1] // new_keys.shape[1]
    scale = 1.0 / math.sqrt(HEAD)
    swap.wait_recv()
    load_out.wait()

    def block(owner):
        at = pl.ds(pl.multiple_of(owner * rows, rows), rows)
        seen = allowed[at, :] > 0.0
        for h in range(kv_heads):
            keys = other_kv[:, 2 * h * HEAD : (2 * h + 1) * HEAD]
            values = other_kv[:, (2 * h + 1) * HEAD : (2 * h + 2) * HEAD]
            fresh_key = new_keys[at, h * HEAD : (h + 1) * HEAD].astype(F32)
            fresh_value = new_values[at, h * HEAD : (h + 1) * HEAD].astype(F32)
            for g in range(shared):
                cols = slice((h * shared + g) * HEAD, (h * shared + g + 1) * HEAD)
                query = queries[at, cols]
                scores = lax.dot_general(
                    query, keys, (((1,), (1,)), ((), ())), preferred_element_type=F32
                )
                scores = jnp.where(seen, scores * scale, -1e30)
                own = jnp.sum(query.astype(F32) * fresh_key, axis=1, keepdims=True) * scale
                top = jnp.maximum(jnp.max(scores, axis=1, keepdims=True), own)
                spread = jnp.where(seen, jnp.exp(scores - top), 0.0)
                self_weight = jnp.exp(own - top)
                total = jnp.sum(spread, axis=1, keepdims=True) + self_weight
                probs = (spread / total).astype(BF16)
                self_prob = (self_weight / total).astype(BF16).astype(F32)
                value = jnp.dot(probs, values, preferred_element_type=F32)
                heads[:, cols] = (value + self_prob * fresh_value).astype(BF16)
        return jnp.dot(heads[...], w_out_here[...], preferred_element_type=F32)

    copies = []
    for j, owner in enumerate((far, right, left)):
        partial[j] = block(owner).astype(BF16)
        copy = pltpu.make_async_remote_copy(
            src_ref=partial.at[j],
            dst_ref=inbox.at[j],
            send_sem=send_sem.at[j],
            recv_sem=recv_sem.at[j],
            device_id={"half": owner},
            device_id_type=MESH,
        )
        copy.start()
        copies.append(copy)
    total = block(x).astype(BF16).astype(F32)
    for j in (1, 2, 0):
        copies[j].wait_recv()
        total = total + inbox[j].astype(F32)
    result[...] = total.astype(BF16)
    swap.wait_send()
    for copy in copies:
        copy.wait_send()


def decode(tok, moe, gain, w_kv, allowed, queries, new_keys, new_values, w_out):
    rows, inner = queries.shape[0] // 4, queries.shape[1]
    wide = w_out.shape[1]
    dma = pltpu.SemaphoreType.DMA
    vmem = pl.BlockSpec(memory_space=pltpu.VMEM)
    hbm = pl.BlockSpec(memory_space=pl.ANY)
    return pl.pallas_call(
        decode_kernel,
        out_shape=jax.ShapeDtypeStruct((rows, wide), BF16),
        in_specs=[vmem, vmem, vmem, hbm, vmem, vmem, vmem, vmem, hbm],
        out_specs=vmem,
        scratch_shapes=[
            pltpu.VMEM(w_kv.shape, BF16),
            pltpu.VMEM(w_out.shape, BF16),
            pltpu.VMEM((tok.shape[0], w_kv.shape[1]), BF16),
            pltpu.VMEM((tok.shape[0], w_kv.shape[1]), BF16),
            pltpu.VMEM((rows, inner), BF16),
            pltpu.VMEM((3, rows, wide), BF16),
            pltpu.VMEM((3, rows, wide), BF16),
            dma((2,)),
            dma,
            dma,
            dma((3,)),
            dma((3,)),
        ],
        compiler_params=pltpu.CompilerParams(
            collective_id=1, has_side_effects=True, vmem_limit_bytes=58 * 2**20
        ),
        cost_estimate=pl.CostEstimate(
            flops=2 * tok.shape[0] * w_kv.size + 8 * rows * w_out.size,
            bytes_accessed=2 * (w_kv.size + w_out.size),
            transcendentals=8 * rows * tok.shape[0] * 8,
        ),
        name="decode",
    )(tok, moe, gain, w_kv, allowed, queries, new_keys, new_values, w_out)


def on_device(
    tokens,
    routes,
    router,
    w_gate,
    w_up,
    w_down,
    norm_gain,
    w_kv,
    lengths,
    queries,
    new_keys,
    new_values,
    w_out,
):
    inputs = tokens[0]
    moe = experts(inputs, routes[0].T, router.T, w_gate[0], w_up[0], w_down[0], RING, 3)
    rows = w_kv.shape[0] // 2
    pool = lax.axis_index("pool")
    mine = lax.dynamic_slice_in_dim(w_kv, pool * rows, rows, 0)
    w_all = lax.all_gather(mine, ("ep", "pool"), axis=0, tiled=True)
    first = lax.dynamic_slice(lengths, (1 - pool, 0, 0), (1, 1, 1))[0]
    second = jnp.arange(inputs.shape[0], dtype=jnp.int32)[None, :] >= first
    prompt = jnp.arange(queries.shape[1], dtype=jnp.int32)[:, None] // SAMPLES
    allowed = (second == (prompt == 1)).astype(F32)
    return decode(
        inputs, moe, norm_gain[None], w_all, allowed, queries[0], new_keys[0], new_values[0], w_out
    )[None]


def solution(mesh):
    in_specs = (
        P("pool", "ep", None),
        P("pool", "ep", None),
        P(),
        P("ep", None, "half"),
        P("ep", None, "half"),
        P("ep", "half", None),
        P(),
        P("ep", "half"),
        P(None, "ep", None),
        P("pool", "ep", "half"),
        P("pool", "ep", "half"),
        P("pool", "ep", "half"),
        P("half", None),
    )
    out_specs = P("pool", ("ep", "half"), None)
    return jax.shard_map(
        on_device, mesh=mesh, in_specs=in_specs, out_specs=out_specs, check_vma=False
    )
```
